32 devices in a mesh: rep: 4 (over z), ep: 8 (over y, x, core).
Axes of the slice: x: 2, y: 2, z: 4, core: 2. Of those that a mesh axis runs over, the one named last changes fastest.
Arguments:
- tokens: bfloat16 [4096, 2048], P(('rep', 'ep')), may hold values from -6 to 6
- experts: int32 [4096, 10], P(('rep', 'ep')), may hold values from 0 to 31, all different within a row; in each aligned block of 128 rows (0 to 127, 128 to 255, ...) at most 64 rows name the same one
- gates: bfloat16 [4096, 10], P(('rep', 'ep')), may hold values from 0.099609375 to 0.5
- w_gate: bfloat16 [32, 2048, 512], P('ep'), may hold values from -0.125 to 0.125
- w_up: bfloat16 [32, 2048, 512], P('ep'), may hold values from -0.125 to 0.125
- w_down: bfloat16 [32, 2048, 512], P('ep'), may hold values from -0.25 to 0.25
Outputs:
- mixed: bfloat16 [4096, 2048], P(('rep', 'ep'))
The draws below stay inside these ranges and needn't reach their ends.
Inputs may be any that keep to these rules, and one draw needn't show every extreme that they name: Each row names 10 different experts. Among the 128 tokens of one device (aligned blocks of rows), no expert is named more than 64 times; in some such blocks one expert is named exactly 64 times.
All inputs are finite; a program needn't handle non-finite values.
Results may differ from the reference program's by a relative error of at most 0.0057.
Values may be sent and summed in bfloat16 or wider, within the bound.
No kernel may reach another device: no remote copies, remote signals or barrier semaphores. Data moves between devices by JAX's collectives and lax.ppermute only.
A program may use at most 128 MiB of HBM per device.

```python
import math
import jax
import jax.numpy as jnp
import numpy as np
from jax import lax

D = 2048
FF = 512
TOPK = 10
TOK_DEV = 128
EXPERTS = 32
CAP = 64
TOKENS = 4096
DEVICES = 32


def steps_of(stream_key, extent, cuts, smallest, largest):
    gain, own = 1.0, jax.random.fold_in(stream_key, 6)
    for axis_at, parts in cuts:
        heights = jnp.exp(jax.random.uniform(jax.random.fold_in(own, axis_at), (parts,), jnp.float32, smallest / len(cuts), largest / len(cuts)))
        gain = gain * jnp.repeat(heights, extent[axis_at] // parts).reshape([-1 if axis == axis_at else 1 for axis in range(len(extent))])
    return gain


def deal_out(rng, own, number, rows, number_of, top, bound, slope):
    sequence = jax.random.permutation(rng, number_of)
    packed, usual = portions_of(number_of, rows * top, bound, slope, True), portions_of(number_of, rows * top, bound, slope, False)
    places = jnp.arange(number_of)

    def named(tallies, rotation):
        used = int((tallies > 0).sum())
        fixed = max(1, used // 4)
        passed = fixed + (places - fixed + rotation * (used - fixed)) % max(1, number_of - fixed)
        return jnp.zeros((number_of,), jnp.int32).at[sequence[jnp.where(places < fixed, places, passed)]].set(jnp.asarray(tallies, jnp.int32))

    tallies = jnp.where(number % 4 == 0, named(packed, number // 4), named(usual, number - number // 4 - 1))
    mixed = jax.random.permutation(jax.random.fold_in(own, 3), number_of)
    giver, receiver = mixed[0:number_of // 2 * 2:2], mixed[1:number_of // 2 * 2:2]
    margin = jnp.minimum(tallies[giver] - 1, bound - tallies[receiver]) // 2
    margin = jnp.where((giver == sequence[0]) | (receiver == sequence[0]) | (tallies[receiver] == 0), 0, jnp.maximum(margin, 0))
    passed = jax.random.randint(jax.random.fold_in(own, 4), (number_of // 2,), 0, 1 << 20) % (margin + 1)
    tallies = tallies.at[giver].add(-passed).at[receiver].add(passed)
    members = jnp.searchsorted(jnp.cumsum(tallies), jnp.arange(rows * top), side="right").astype(jnp.int32)
    listing = members.reshape(top, rows).T
    listing = listing[jax.random.permutation(jax.random.fold_in(own, 1), rows)]
    rotation = jax.random.randint(jax.random.fold_in(own, 2), (rows, 1), 0, top)
    return jnp.take_along_axis(listing, (jnp.arange(top)[None, :] + rotation) % top, axis=1)


def portions_of(number_of, total, bound, skew, full):
    portions = [(1 << 20) // math.isqrt(rank ** skew) + 1 for rank in range(1, number_of + 1)]
    largest = bound if full else min(bound, max(-(-total // number_of), total * portions[0] // sum(portions)))
    least = 1 if total - largest >= number_of - 1 else 0
    given, spare = [largest] + [least] * (number_of - 1), total - largest - least * (number_of - 1)
    while spare > 0:
        movable = [i for i in range(1, number_of) if given[i] < largest] or [i for i in range(1, number_of) if given[i] < bound]
        whole, remaining = sum([portions[i] for i in movable]), spare
        for i in movable:
            addition = min(bound - given[i], max(1, remaining * portions[i] // whole), spare)
            given[i] = given[i] + addition
            spare = spare - addition
    return np.array(given)


def bell_draw(stream_key, extent, spread, reach, shards=(), held_as=jnp.bfloat16):
    drawn = jax.random.normal(stream_key, extent, jnp.float32) * spread
    if len(shards) > 0:
        drawn = steps_of(stream_key, extent, shards, -0.22, 0.18) * drawn
    return jnp.clip(drawn, min=-reach, max=reach).astype(held_as)


def setup_inputs(seed: int = 0) -> dict:
    splits = jax.random.split(jax.random.key(seed), 7)
    tokens = bell_draw(splits[0], (TOKENS, D), 1.0, 6.0, ((0, 32),))
    experts_keys = jax.random.split(jax.random.fold_in(splits[1], 1), TOKENS // TOK_DEV)
    experts_turns = jax.random.permutation(jax.random.fold_in(splits[1], 3), TOKENS // TOK_DEV)
    experts = jax.vmap(lambda own, number: deal_out(jax.random.fold_in(splits[1], 2), own, number, TOK_DEV, EXPERTS, TOPK, CAP, 2))(experts_keys, experts_turns).reshape((TOKENS, TOPK))
    gates = jnp.clip(0.099609375 + 0.40039062 * jax.random.uniform(splits[2], (TOKENS, TOPK), jnp.float32) ** steps_of(splits[2], (TOKENS, TOPK), ((0, 32),), -0.2, 0.2), 0.099609375, 0.5).astype(jnp.bfloat16)
    w_gate = bell_draw(splits[3], (EXPERTS, D, FF), D ** -0.5, 0.125, ((0, 8),))
    w_up = bell_draw(splits[4], (EXPERTS, D, FF), D ** -0.5, 0.125, ((0, 8),))
    w_down = bell_draw(splits[5], (EXPERTS, D, FF), FF ** -0.5, 0.25, ((0, 8),))
    return {"tokens": tokens, "experts": experts, "gates": gates, "w_gate": w_gate, "w_up": w_up, "w_down": w_down}


def reference(tokens, experts, gates, w_gate, w_up, w_down):
    flat = experts.reshape(DEVICES, TOK_DEV * TOPK)
    onehot = (flat[:, :, None] == jnp.arange(EXPERTS, dtype=jnp.int32)[None, None, :]).astype(jnp.int32)
    position = jnp.sum(jnp.cumsum(onehot, axis=1) * onehot, axis=-1) - 1
    rows_each = DEVICES * CAP
    owner = jnp.arange(DEVICES, dtype=jnp.int32)[:, None]
    slot = (flat * rows_each + owner * CAP + position).reshape(-1).astype(jnp.int32)
    token_ids = (jnp.arange(DEVICES * TOK_DEV * TOPK, dtype=jnp.int32) // TOPK).astype(jnp.int32)
    table = jnp.zeros((EXPERTS * rows_each,), jnp.int32).at[slot].set(token_ids).reshape(EXPERTS, rows_each)
    weights = jnp.zeros((EXPERTS * rows_each,), jnp.float32).at[slot].set(gates.reshape(-1).astype(jnp.float32)).reshape(EXPERTS, rows_each)

    def one_expert(total, index):
        picked = tokens[table[index]]
        gate_act = jnp.dot(picked, w_gate[index], preferred_element_type=jnp.float32)
        up_act = jnp.dot(picked, w_up[index], preferred_element_type=jnp.float32)
        hidden = (jax.nn.silu(gate_act) * up_act).astype(jnp.bfloat16)
        result = jnp.dot(hidden, w_down[index].T, preferred_element_type=jnp.float32).astype(jnp.bfloat16)
        contrib = result.astype(jnp.float32) * weights[index][:, None]
        return total.at[table[index]].add(contrib), None

    start = jnp.zeros((TOKENS, D), jnp.float32)
    total, unused = lax.scan(one_expert, start, jnp.arange(EXPERTS, dtype=jnp.int32))
    return total.astype(jnp.bfloat16)
```

```python
import functools

import jax
import jax.numpy as jnp
from jax import lax
from jax.experimental import pallas as pl
from jax.experimental.pallas import tpu as pltpu
from jax.sharding import PartitionSpec as P

MIB = 2**20
LANES = 128
NT = (((1,), (1,)), ((), ()))
VMEM_SPEC = pl.BlockSpec(memory_space=pltpu.VMEM)
ANY_SPEC = pl.BlockSpec(memory_space=pl.ANY)


def flip(x, mask):
    n = lax.axis_size("ep")
    return lax.ppermute(x, "ep", [(i, i ^ mask) for i in range(n)])


def prepare_kernel(tokens, experts, gates, out, table, sems):
    width = tokens.shape[1]
    rows = pltpu.make_async_copy(tokens, out.at[:, pl.ds(0, width)], sems.at[0])
    rows.start()
    lanes, count = table.shape[1], table.shape[0]
    ids = lax.broadcasted_iota(jnp.int32, (lanes, count), 0)
    chosen = experts[...]
    weight = gates[...].astype(jnp.float32)
    total = jnp.zeros((lanes, count), jnp.float32)
    for k in range(chosen.shape[0]):
        total += jnp.where(ids == chosen[k : k + 1, :], weight[k : k + 1, :], 0.0)
    table[...] = total.T.astype(jnp.bfloat16)
    last = pltpu.make_async_copy(table, out.at[:, pl.ds(width, lanes)], sems.at[1])
    last.start()
    rows.wait()
    last.wait()


def prepare(tokens, experts, gates, lanes):
    count, width = tokens.shape
    return pl.pallas_call(
        prepare_kernel,
        in_specs=[ANY_SPEC, VMEM_SPEC, VMEM_SPEC],
        out_specs=ANY_SPEC,
        out_shape=jax.ShapeDtypeStruct((count, width + lanes), jnp.bfloat16),
        scratch_shapes=[pltpu.VMEM((count, lanes), jnp.bfloat16), pltpu.SemaphoreType.DMA((2,))],
        name="prepare",
    )(tokens, experts.T, gates.T)


def hidden_of(rows, gate_w, up_w, weight):
    gate_act = jnp.dot(rows, gate_w, preferred_element_type=jnp.float32)
    up_act = jnp.dot(rows, up_w, preferred_element_type=jnp.float32)
    return (gate_act / (1.0 + jnp.exp(-gate_act)) * up_act * weight).astype(jnp.bfloat16)


def gather_inputs(first, second, rows, held):
    count = first.shape[0]
    width = rows.shape[1]
    rows[:count] = first[:, :width]
    rows[count:] = second[:, :width]
    table = jnp.concatenate([first[:, width:], second[:, width:]], axis=0).astype(jnp.float32)
    lane = lax.broadcasted_iota(jnp.int32, table.shape, 1)
    base = lax.axis_index("ep") * held
    return [
        jnp.sum(jnp.where(lane == base + e, table, 0.0), axis=1, keepdims=True) for e in range(held)
    ]


def down_all(hidden, w_down, mine, other, tile=512):
    held, width, units = w_down.shape
    count = mine.shape[0]
    for start in range(0, width, tile):
        total = None
        for e in range(held):
            part = lax.dot_general(
                hidden[:, e * units : (e + 1) * units],
                w_down[e, start : start + tile, :],
                NT,
                preferred_element_type=jnp.float32,
            )
            total = part if total is None else total + part
        total = total.astype(jnp.bfloat16)
        mine[:, start : start + tile] = total[:count]
        other[:, start : start + tile] = total[count:]


def first_kernel(first, second, gate_hbm, up_hbm, down_hbm, mine, other, w_gate, w_up, w_down, rows, hidden, sems):
    held, _, units = w_gate.shape
    order = [(gate_hbm, w_gate, e, 0) for e in range(held)]
    order = [c for e in range(held) for c in ((gate_hbm, w_gate, e, 0), (up_hbm, w_up, e, 1))]
    order += [(down_hbm, w_down, e, 2) for e in range(held)]
    copies = {}
    for src, dst, e, which in order:
        copies[e, which] = pltpu.make_async_copy(src.at[e], dst.at[e], sems.at[which, e])
        copies[e, which].start()
    weights = gather_inputs(first, second, rows, held)
    for e in range(held):
        copies[e, 0].wait()
        copies[e, 1].wait()
        hidden[:, e * units : (e + 1) * units] = hidden_of(rows[...], w_gate[e], w_up[e], weights[e])
    for e in range(held):
        copies[e, 2].wait()
    down_all(hidden, w_down, mine, other)


def chunk_kernel(first, second, w_gate, w_up, w_down, mine, other, rows, hidden):
    held, _, units = w_gate.shape
    weights = gather_inputs(first, second, rows, held)
    for e in range(held):
        hidden[:, e * units : (e + 1) * units] = hidden_of(rows[...], w_gate[e], w_up[e], weights[e])
    down_all(hidden, w_down, mine, other)


def scratch_of(first, w_gate):
    count = first.shape[0]
    held, width, units = w_gate.shape
    return [pltpu.VMEM((2 * count, width), jnp.bfloat16), pltpu.VMEM((2 * count, held * units), jnp.bfloat16)]


def cost_of(first, w_gate):
    held, width, units = w_gate.shape
    flops = 2 * 2 * first.shape[0] * 3 * held * width * units
    return pl.CostEstimate(flops=flops, bytes_accessed=4 * first.size, transcendentals=0)


def first_chunk(first, second, w_gate, w_up, w_down):
    half = jax.ShapeDtypeStruct((first.shape[0], w_gate.shape[1]), jnp.bfloat16)
    kept = [pltpu.VMEM(w.shape, w.dtype) for w in (w_gate, w_up, w_down)]
    return pl.pallas_call(
        first_kernel,
        in_specs=[VMEM_SPEC] * 2 + [ANY_SPEC] * 3,
        out_specs=[VMEM_SPEC] * 5,
        out_shape=[half, half] + kept,
        scratch_shapes=scratch_of(first, w_gate) + [pltpu.SemaphoreType.DMA((3, w_gate.shape[0]))],
        compiler_params=pltpu.CompilerParams(vmem_limit_bytes=16 * MIB),
        cost_estimate=cost_of(first, w_gate),
        name="first_chunk",
    )(first, second, w_gate, w_up, w_down)


def chunk(first, second, weights):
    half = jax.ShapeDtypeStruct((first.shape[0], weights[0].shape[1]), jnp.bfloat16)
    return pl.pallas_call(
        chunk_kernel,
        in_specs=[VMEM_SPEC] * 5,
        out_specs=[VMEM_SPEC] * 2,
        out_shape=[half, half],
        scratch_shapes=scratch_of(first, weights[0]),
        compiler_params=pltpu.CompilerParams(vmem_limit_bytes=16 * MIB),
        cost_estimate=cost_of(first, weights[0]),
        name="chunk",
    )(first, second, *weights)


def body(tokens, experts, gates, w_gate, w_up, w_down):
    n_ep = lax.axis_size("ep")
    n_experts = w_gate.shape[0] * n_ep
    lanes = -(-n_experts // LANES) * LANES
    mixed_rows = prepare(tokens, experts, gates, lanes)
    arrived = {d: flip(mixed_rows, 2 * d) for d in range(1, n_ep // 2)}
    mine, other, *weights = first_chunk(mixed_rows, flip(mixed_rows, 1), w_gate, w_up, w_down)
    total = mine.astype(jnp.float32) + flip(other, 1).astype(jnp.float32)
    returned = []
    for d, rows in arrived.items():
        mine, other = chunk(rows, flip(rows, 1), weights)
        pair = mine.astype(jnp.float32) + flip(other, 1).astype(jnp.float32)
        returned.append(flip(pair.astype(jnp.bfloat16), 2 * d))
    for part in returned:
        total = total + part.astype(jnp.float32)
    return total.astype(jnp.bfloat16)


def solution(mesh):
    in_specs = (
        P(("rep", "ep"), None),
        P(("rep", "ep"), None),
        P(("rep", "ep"), None),
        P("ep", None, None),
        P("ep", None, None),
        P("ep", None, None),
    )
    out_specs = P(("rep", "ep"), None)
    return jax.shard_map(body, mesh=mesh, in_specs=in_specs, out_specs=out_specs, check_vma=False)
```

```python
import functools

import jax
import jax.numpy as jnp
from jax import lax
from jax.experimental import pallas as pl
from jax.experimental.pallas import tpu as pltpu
from jax.sharding import PartitionSpec as P

MIB = 2**20
LANES = 128
NT = (((1,), (1,)), ((), ()))
VMEM_SPEC = pl.BlockSpec(memory_space=pltpu.VMEM)
HBM_SPEC = pl.BlockSpec(memory_space=pltpu.HBM)
CORE = 1


def flip(x, mask):
    n = lax.axis_size("ep")
    return lax.ppermute(x, "ep", [(i, i ^ mask) for i in range(n)])


def after(x, *others):
    return lax.optimization_barrier((x, *others))[0]


def in_vmem(*arrays):
    return [pltpu.with_memory_space_constraint(a, pltpu.VMEM) for a in arrays]


def in_hbm(*arrays):
    return [pltpu.with_memory_space_constraint(a, pltpu.HBM) for a in arrays]


def params(limit=16):
    return pltpu.CompilerParams(vmem_limit_bytes=limit * MIB)


def prepare_kernel(tokens, experts, gates, whole, low, high, chosen, weight, sems):
    count, width = tokens.shape
    half = count // 2
    lanes = whole.shape[1] - width
    copies = [
        pltpu.make_async_copy(experts, chosen, sems.at[0]),
        pltpu.make_async_copy(gates, weight, sems.at[1]),
        pltpu.make_async_copy(tokens.at[pl.ds(0, half)], low.at[:, pl.ds(0, width)], sems.at[2]),
        pltpu.make_async_copy(tokens.at[pl.ds(half, half)], high.at[:, pl.ds(0, width)], sems.at[3]),
        pltpu.make_async_copy(tokens, whole.at[:, pl.ds(0, width)], sems.at[4]),
    ]
    for copy in copies:
        copy.start()
    copies[0].wait()
    copies[1].wait()
    ids = lax.broadcasted_iota(jnp.int32, (lanes, count), 0)
    total = jnp.zeros((lanes, count), jnp.float32)
    for k in range(chosen.shape[0]):
        gate = weight[k : k + 1, :].astype(jnp.float32)
        total += jnp.where(ids == chosen[k : k + 1, :], gate, 0.0)
    table = total.T.astype(jnp.bfloat16)
    whole[:, width:] = table
    low[:, width:] = table[:half]
    high[:, width:] = table[half:]
    for copy in copies[2:]:
        copy.wait()


def prepare(tokens, experts, gates, lanes):
    count, width = tokens.shape
    rows = [(count, width + lanes), (count // 2, width + lanes), (count // 2, width + lanes)]
    return pl.pallas_call(
        prepare_kernel,
        in_specs=[HBM_SPEC] * 3,
        out_specs=[VMEM_SPEC] * 3,
        out_shape=[pltpu.VMEM(shape, jnp.bfloat16) for shape in rows],
        scratch_shapes=[
            pltpu.VMEM(experts.shape[::-1], jnp.int32),
            pltpu.VMEM(gates.shape[::-1], jnp.bfloat16),
            pltpu.SemaphoreType.DMA((5,)),
        ],
        compiler_params=params(4),
        name="prepare",
    )(*in_hbm(tokens, experts.T, gates.T))


def gather_inputs(parts, rows, held):
    width = rows.shape[1]
    tables, start = [], 0
    for part in parts:
        rows[start : start + part.shape[0]] = part[:, :width]
        tables.append(part[:, width:])
        start += part.shape[0]
    table = jnp.concatenate(tables, axis=0).astype(jnp.float32)
    lane = lax.broadcasted_iota(jnp.int32, table.shape, 1)
    base = lax.axis_index("ep") * held
    return [
        jnp.sum(jnp.where(lane == base + e, table, 0.0), axis=1, keepdims=True) for e in range(held)
    ]


def hidden_of(rows, gate_w, up_w, weight):
    gate_act = jnp.dot(rows, gate_w, preferred_element_type=jnp.float32)
    up_act = jnp.dot(rows, up_w, preferred_element_type=jnp.float32)
    return (gate_act / (1.0 + jnp.exp(-gate_act)) * up_act * weight).astype(jnp.bfloat16)


def down_all(hidden, w_down, mine, other, tile=512):
    held, width, units = w_down.shape
    count = mine.shape[0]
    for start in range(0, width, tile):
        total = None
        for e in range(held):
            part = lax.dot_general(
                hidden[:, e * units : (e + 1) * units],
                w_down[e, start : start + tile, :],
                NT,
                preferred_element_type=jnp.float32,
            )
            total = part if total is None else total + part
        total = total.astype(jnp.bfloat16)
        mine[:, start : start + tile] = total[:count]
        other[:, start : start + tile] = total[count:]


def load_kernel(own, twin, gate_hbm, up_hbm, w_gate, w_up, hidden, rows, sems):
    held, _, units = w_gate.shape
    copies = []
    for e in range(held):
        for which, (src, dst) in enumerate(((gate_hbm, w_gate), (up_hbm, w_up))):
            copies.append(pltpu.make_async_copy(src.at[e], dst.at[e], sems.at[which, e]))
            copies[-1].start()
    weights = gather_inputs([own, twin], rows, held)
    for e in range(held):
        copies[2 * e].wait()
        copies[2 * e + 1].wait()
        hidden[:, e * units : (e + 1) * units] = hidden_of(rows[...], w_gate[e], w_up[e], weights[e])


def load(own, twin, w_gate, w_up):
    count = 2 * own.shape[0]
    held, width, units = w_gate.shape
    return pl.pallas_call(
        load_kernel,
        in_specs=[VMEM_SPEC] * 2 + [HBM_SPEC] * 2,
        out_specs=[VMEM_SPEC] * 3,
        out_shape=[pltpu.VMEM(w_gate.shape, w_gate.dtype)] * 2 + [pltpu.VMEM((count, held * units), jnp.bfloat16)],
        scratch_shapes=[pltpu.VMEM((count, width), jnp.bfloat16), pltpu.SemaphoreType.DMA((2, held))],
        compiler_params=params(),
        name="load",
    )(own, twin, *in_hbm(w_gate, w_up))


def first_kernel(*refs, parts):
    inputs, (w_gate, w_up, down_hbm, mine, other, w_down, rows, hidden, sem) = refs[:parts], refs[parts:]
    copy = pltpu.make_async_copy(down_hbm, w_down, sem)
    copy.start()
    held, _, units = w_gate.shape
    weights = gather_inputs(inputs, rows, held)
    for e in range(held):
        hidden[:, e * units : (e + 1) * units] = hidden_of(rows[...], w_gate[e], w_up[e], weights[e])
    copy.wait()
    down_all(hidden, w_down, mine, other)


def chunk_kernel(*refs, parts):
    inputs, (w_gate, w_up, w_down, mine, other, rows, hidden) = refs[:parts], refs[parts:]
    held, _, units = w_gate.shape
    weights = gather_inputs(inputs, rows, held)
    for e in range(held):
        hidden[:, e * units : (e + 1) * units] = hidden_of(rows[...], w_gate[e], w_up[e], weights[e])
    down_all(hidden, w_down, mine, other)


def shapes_of(parts, w_gate):
    count = sum(part.shape[0] for part in parts)
    held, width, units = w_gate.shape
    halves = [pltpu.VMEM((count // 2, width), jnp.bfloat16)] * 2
    scratch = [pltpu.VMEM((count, width), jnp.bfloat16), pltpu.VMEM((count, held * units), jnp.bfloat16)]
    return halves, scratch


def first_chunk(parts, w_gate, w_up, w_down):
    halves, scratch = shapes_of(parts, w_gate)
    return pl.pallas_call(
        functools.partial(first_kernel, parts=len(parts)),
        in_specs=[VMEM_SPEC] * (len(parts) + 2) + [HBM_SPEC],
        out_specs=[VMEM_SPEC] * 3,
        out_shape=halves + [pltpu.VMEM(w_down.shape, w_down.dtype)],
        scratch_shapes=scratch + [pltpu.SemaphoreType.DMA],
        compiler_params=params(),
        name="first_chunk",
    )(*in_vmem(*parts, w_gate, w_up), *in_hbm(w_down))


def chunk(parts, w_gate, w_up, w_down):
    halves, scratch = shapes_of(parts, w_gate)
    return pl.pallas_call(
        functools.partial(chunk_kernel, parts=len(parts)),
        in_specs=[VMEM_SPEC] * (len(parts) + 3),
        out_specs=[VMEM_SPEC] * 2,
        out_shape=halves,
        scratch_shapes=scratch,
        compiler_params=params(),
        name="chunk",
    )(*in_vmem(*parts, w_gate, w_up, w_down))


def finish_own(hidden, w_down):
    half = pltpu.VMEM((hidden.shape[0] // 2, w_down.shape[1]), jnp.bfloat16)
    return pl.pallas_call(
        down_all,
        in_specs=[VMEM_SPEC] * 2,
        out_specs=[VMEM_SPEC] * 2,
        out_shape=[half, half],
        compiler_params=params(),
        name="finish_own",
    )(*in_vmem(hidden, w_down))


def add_kernel(*refs):
    *inputs, low, high = refs
    half = low.shape[0]
    for out, block in ((low, slice(0, half)), (high, slice(half, 2 * half))):
        total = inputs[0][block].astype(jnp.float32)
        for part in inputs[1:]:
            total += part[block].astype(jnp.float32)
        out[...] = total.astype(out.dtype)


def add_halves(first, second):
    half = pltpu.VMEM((first.shape[0] // 2, first.shape[1]), first.dtype)
    return pl.pallas_call(
        add_kernel,
        in_specs=[VMEM_SPEC] * 2,
        out_specs=[VMEM_SPEC] * 2,
        out_shape=[half, half],
        compiler_params=params(8),
        name="add_halves",
    )(*in_vmem(first, second))


def add_relay_kernel(first, second, low_relay, high_relay, low, high):
    half = low.shape[0]
    for out, relay, block in ((low, low_relay, slice(0, half)), (high, high_relay, slice(half, 2 * half))):
        total = first[block].astype(jnp.float32) + second[block].astype(jnp.float32)
        out[...] = (total + relay[...].astype(jnp.float32)).astype(out.dtype)


def add_relay(first, second, low_relay, high_relay):
    half = pltpu.VMEM(low_relay.shape, first.dtype)
    return pl.pallas_call(
        add_relay_kernel,
        in_specs=[VMEM_SPEC] * 4,
        out_specs=[VMEM_SPEC] * 2,
        out_shape=[half, half],
        compiler_params=params(8),
        name="add_relay",
    )(*in_vmem(first, second, low_relay, high_relay))


def finish_kernel(mine, twin, low_parts, high_parts, out):
    half = low_parts[0].shape[0]
    for parts, block in ((low_parts, slice(0, half)), (high_parts, slice(half, 2 * half))):
        total = mine[block].astype(jnp.float32) + twin[block].astype(jnp.float32)
        for part in parts:
            total += part[...].astype(jnp.float32)
        out[block] = total.astype(out.dtype)


def finish(mine, twin, low_parts, high_parts):
    parts = [*low_parts, *high_parts]

    def kernel(mine, twin, *refs):
        finish_kernel(mine, twin, refs[: len(low_parts)], refs[len(low_parts) : -1], refs[-1])

    return pl.pallas_call(
        kernel,
        in_specs=[VMEM_SPEC] * (2 + len(parts)),
        out_specs=VMEM_SPEC,
        out_shape=jax.ShapeDtypeStruct(mine.shape, mine.dtype),
        compiler_params=params(8),
        name="finish",
    )(*in_vmem(mine, twin, *parts))


def on_four_chips(whole, low, high, w_gate, w_up, w_down):
    x, y = 2, 4
    near_x, near_y = flip(low, x), flip(high, y)
    w_gate, w_up, hidden = load(whole, flip(whole, CORE), w_gate, w_up)
    near_x, near_y, hidden = lax.optimization_barrier((near_x, near_y, hidden))
    far_low, far_high = flip(near_x, y), flip(near_y, x)
    parts = [near_x, near_y, flip(near_x, CORE), flip(near_y, CORE)]
    low, high = lax.optimization_barrier((low, high, near_x, near_y))[:2]
    next_x, next_y = flip(high, x), flip(low, y)
    mine_near, other_near, w_down = first_chunk(parts, w_gate, w_up, w_down)
    weights = (w_gate, w_up, w_down)
    far_low, far_high, hidden, _ = lax.optimization_barrier((far_low, far_high, hidden, mine_near))
    parts = [far_low, far_high, flip(far_low, CORE), flip(far_high, CORE)]
    mine_own, other_own = finish_own(hidden, w_down)
    twin_own = flip(other_own, CORE)
    sum_x, sum_y = add_halves(mine_near, flip(other_near, CORE))
    back_x, back_y = flip(sum_x, x), flip(sum_y, y)
    mine_far, other_far = chunk([after(parts[0], mine_own), *parts[1:]], *weights)
    next_x, next_y, _ = lax.optimization_barrier((next_x, next_y, mine_far))
    relay_low, relay_high = add_halves(mine_far, flip(other_far, CORE))
    relay_low, relay_high = flip(relay_low, x), flip(relay_high, y)
    mine_next, other_next = chunk([next_x, next_y, flip(next_x, CORE), flip(next_y, CORE)], *weights)
    sum_x, sum_y = add_relay(mine_next, flip(other_next, CORE), relay_high, relay_low)
    last_x, last_y = flip(sum_x, x), flip(sum_y, y)
    return finish(mine_own, twin_own, [back_x, last_y], [back_y, last_x])


def on_any_chips(whole, low, high, w_gate, w_up, w_down):
    offsets = range(2, lax.axis_size("ep"), 2)
    arrived = [flip(whole, d) for d in offsets]
    w_gate, w_up, hidden = load(whole, flip(whole, CORE), w_gate, w_up)
    low_parts, high_parts = [], []
    weights = None
    for d, rows in zip(offsets, arrived):
        parts = [rows, flip(rows, CORE)]
        if weights is None:
            mine, other, w_down = first_chunk(parts, w_gate, w_up, w_down)
            weights = (w_gate, w_up, w_down)
        else:
            mine, other = chunk(parts, *weights)
        low, high = add_halves(mine, flip(other, CORE))
        low_parts.append(flip(low, d))
        high_parts.append(flip(high, d))
    mine, other = finish_own(hidden, w_down)
    return finish(mine, flip(other, CORE), low_parts, high_parts)


def body(tokens, experts, gates, w_gate, w_up, w_down):
    n_ep = lax.axis_size("ep")
    n_experts = w_gate.shape[0] * n_ep
    lanes = -(-n_experts // LANES) * LANES
    whole, low, high = prepare(tokens, experts, gates, lanes)
    run = on_four_chips if n_ep == 8 else on_any_chips
    return run(whole, low, high, w_gate, w_up, w_down)


def solution(mesh):
    in_specs = (
        P(("rep", "ep"), None),
        P(("rep", "ep"), None),
        P(("rep", "ep"), None),
        P("ep", None, None),
        P("ep", None, None),
        P("ep", None, None),
    )
    out_specs = P(("rep", "ep"), None)
    return jax.shard_map(body, mesh=mesh, in_specs=in_specs, out_specs=out_specs, check_vma=False)
```

```python
import functools

import jax
import jax.numpy as jnp
from jax import lax
from jax.experimental import pallas as pl
from jax.experimental.pallas import tpu as pltpu
from jax.sharding import PartitionSpec as P

MIB = 2**20
LANES = 128
NT = (((1,), (1,)), ((), ()))
VMEM_SPEC = pl.BlockSpec(memory_space=pltpu.VMEM)
HBM_SPEC = pl.BlockSpec(memory_space=pltpu.HBM)
CORE = 1
COST = pl.CostEstimate(flops=0, bytes_accessed=0, transcendentals=0)


def flip(x, mask):
    n = lax.axis_size("ep")
    return lax.ppermute(x, "ep", [(i, i ^ mask) for i in range(n)])


def after(x, *others):
    return lax.optimization_barrier((x, *others))[0]


def in_vmem(*arrays):
    return [pltpu.with_memory_space_constraint(a, pltpu.VMEM) for a in arrays]


def in_hbm(*arrays):
    return [pltpu.with_memory_space_constraint(a, pltpu.HBM) for a in arrays]


def params(limit=6):
    return pltpu.CompilerParams(vmem_limit_bytes=limit * MIB)


def prepare_kernel(tokens, experts, gates, whole, low, high, chosen, weight, sems):
    count, width = tokens.shape
    half = count // 2
    lanes = whole.shape[1] - width
    copies = [
        pltpu.make_async_copy(experts, chosen, sems.at[0]),
        pltpu.make_async_copy(gates, weight, sems.at[1]),
        pltpu.make_async_copy(tokens.at[pl.ds(0, half)], low.at[:, pl.ds(0, width)], sems.at[2]),
        pltpu.make_async_copy(tokens.at[pl.ds(half, half)], high.at[:, pl.ds(0, width)], sems.at[3]),
        pltpu.make_async_copy(tokens, whole.at[:, pl.ds(0, width)], sems.at[4]),
    ]
    for copy in copies:
        copy.start()
    copies[0].wait()
    copies[1].wait()
    ids = lax.broadcasted_iota(jnp.int32, (lanes, count), 0)
    total = jnp.zeros((lanes, count), jnp.float32)
    for k in range(chosen.shape[0]):
        gate = weight[k : k + 1, :].astype(jnp.float32)
        total += jnp.where(ids == chosen[k : k + 1, :], gate, 0.0)
    table = total.T.astype(jnp.bfloat16)
    whole[:, width:] = table
    low[:, width:] = table[:half]
    high[:, width:] = table[half:]
    for copy in copies[2:]:
        copy.wait()


def prepare(tokens, experts, gates, lanes):
    count, width = tokens.shape
    rows = [(count, width + lanes), (count // 2, width + lanes), (count // 2, width + lanes)]
    return pl.pallas_call(
        prepare_kernel,
        in_specs=[HBM_SPEC] * 3,
        out_specs=[VMEM_SPEC] * 3,
        out_shape=[pltpu.VMEM(shape, jnp.bfloat16) for shape in rows],
        scratch_shapes=[
            pltpu.VMEM(experts.shape[::-1], jnp.int32),
            pltpu.VMEM(gates.shape[::-1], jnp.bfloat16),
            pltpu.SemaphoreType.DMA((5,)),
        ],
        cost_estimate=pl.CostEstimate(flops=10**11, bytes_accessed=10**8, transcendentals=0),
        compiler_params=params(4),
        name="prepare",
    )(*in_hbm(tokens, experts.T, gates.T))


def gather_inputs(parts, rows, held):
    width = rows.shape[1]
    tables, start = [], 0
    for part in parts:
        rows[start : start + part.shape[0]] = part[:, :width]
        tables.append(part[:, width:])
        start += part.shape[0]
    table = jnp.concatenate(tables, axis=0).astype(jnp.float32)
    lane = lax.broadcasted_iota(jnp.int32, table.shape, 1)
    base = lax.axis_index("ep") * held
    return [
        jnp.sum(jnp.where(lane == base + e, table, 0.0), axis=1, keepdims=True) for e in range(held)
    ]


def hidden_of(rows, gate_w, up_w, weight):
    gate_act = jnp.dot(rows, gate_w, preferred_element_type=jnp.float32)
    up_act = jnp.dot(rows, up_w, preferred_element_type=jnp.float32)
    return (gate_act / (1.0 + jnp.exp(-gate_act)) * up_act * weight).astype(jnp.bfloat16)


def down_all(hidden, w_down, mine, *others, tile=512):
    held, width, units = w_down.shape
    count, piece = mine.shape[0], others[0].shape[0]
    for start in range(0, width, tile):
        total = None
        for e in range(held):
            part = lax.dot_general(
                hidden[:, e * units : (e + 1) * units],
                w_down[e, start : start + tile, :],
                NT,
                preferred_element_type=jnp.float32,
            )
            total = part if total is None else total + part
        total = total.astype(jnp.bfloat16)
        mine[:, start : start + tile] = total[:count]
        for i, other in enumerate(others):
            first = count + i * piece
            other[:, start : start + tile] = total[first : first + piece]


def hidden_kernel(*refs, parts):
    inputs, (w_gate, w_up, hidden, rows) = refs[:parts], refs[parts:]
    held, _, units = w_gate.shape
    weights = gather_inputs(inputs, rows, held)
    for e in range(held):
        hidden[:, e * units : (e + 1) * units] = hidden_of(rows[...], w_gate[e], w_up[e], weights[e])


def hidden_units(parts, w_gate, w_up):
    count = sum(part.shape[0] for part in parts)
    held, width, units = w_gate.shape
    return pl.pallas_call(
        functools.partial(hidden_kernel, parts=len(parts)),
        in_specs=[VMEM_SPEC] * (len(parts) + 2),
        out_specs=VMEM_SPEC,
        out_shape=pltpu.VMEM((count, held * units), jnp.bfloat16),
        scratch_shapes=[pltpu.VMEM((count, width), jnp.bfloat16)],
        cost_estimate=COST,
        compiler_params=params(),
        name="hidden_units",
    )(*in_vmem(*parts, w_gate, w_up))


def chunk_kernel(*refs, parts):
    inputs, (w_gate, w_up, w_down), refs = refs[:parts], refs[parts : parts + 3], refs[parts + 3 :]
    mine, *others, rows, hidden = refs
    held, _, units = w_gate.shape
    weights = gather_inputs(inputs, rows, held)
    for e in range(held):
        hidden[:, e * units : (e + 1) * units] = hidden_of(rows[...], w_gate[e], w_up[e], weights[e])
    down_all(hidden, w_down, mine, *others)


def sum_shapes(count, width, pieces):
    pieces = [pltpu.VMEM((count // 2 // pieces, width), jnp.bfloat16)] * pieces
    return [pltpu.VMEM((count // 2, width), jnp.bfloat16), *pieces]


def scratch_of(count, w_gate):
    held, width, units = w_gate.shape
    return [pltpu.VMEM((count, width), jnp.bfloat16), pltpu.VMEM((count, held * units), jnp.bfloat16)]


def chunk(parts, w_gate, w_up, w_down, pieces=1):
    count = sum(part.shape[0] for part in parts)
    mine, *others = pl.pallas_call(
        functools.partial(chunk_kernel, parts=len(parts)),
        in_specs=[VMEM_SPEC] * (len(parts) + 3),
        out_specs=[VMEM_SPEC] * (1 + pieces),
        out_shape=sum_shapes(count, w_gate.shape[1], pieces),
        scratch_shapes=scratch_of(count, w_gate),
        cost_estimate=COST,
        compiler_params=params(),
        name="chunk",
    )(*in_vmem(*parts, w_gate, w_up, w_down))
    return mine, others


def down_units(hidden, w_down, pieces=1):
    mine, *others = pl.pallas_call(
        down_all,
        in_specs=[VMEM_SPEC] * 2,
        out_specs=[VMEM_SPEC] * (1 + pieces),
        out_shape=sum_shapes(hidden.shape[0], w_down.shape[1], pieces),
        cost_estimate=COST,
        compiler_params=params(),
        name="down_units",
    )(*in_vmem(hidden, w_down))
    return mine, others


def swap(others):
    return [flip(other, CORE) for other in others]


def add_kernel(mine, *refs):
    *twins, low, high = refs
    half, piece = low.shape[0], twins[0].shape[0]
    step = min(half, piece)
    for first in range(0, 2 * half, step):
        out, at = (low, first) if first < half else (high, first - half)
        twin = twins[first // piece][first % piece : first % piece + step]
        total = mine[first : first + step].astype(jnp.float32) + twin.astype(jnp.float32)
        out[at : at + step] = total.astype(out.dtype)


def add_halves(mine, twins):
    half = pltpu.VMEM((mine.shape[0] // 2, mine.shape[1]), jnp.bfloat16)
    return pl.pallas_call(
        add_kernel,
        in_specs=[VMEM_SPEC] * (1 + len(twins)),
        out_specs=[VMEM_SPEC] * 2,
        out_shape=[half, half],
        cost_estimate=COST,
        compiler_params=params(8),
        name="add_halves",
    )(*in_vmem(mine, *twins))


def add_relay_kernel(mine, low, high, out):
    half = low.shape[0]
    out[:half] = mine[:half].astype(jnp.float32) + low[...].astype(jnp.float32)
    out[half:] = mine[half:].astype(jnp.float32) + high[...].astype(jnp.float32)


def add_relay(mine, low, high):
    return pl.pallas_call(
        add_relay_kernel,
        in_specs=[VMEM_SPEC] * 3,
        out_specs=VMEM_SPEC,
        out_shape=pltpu.VMEM(mine.shape, jnp.float32),
        cost_estimate=COST,
        compiler_params=params(8),
        name="add_relay",
    )(*in_vmem(mine, low, high))


def join_kernel(first, second, out):
    half = first.shape[0]
    out[:half] = first[...]
    out[half:] = second[...]


def join(first, second):
    return pl.pallas_call(
        join_kernel,
        in_specs=[VMEM_SPEC] * 2,
        out_specs=VMEM_SPEC,
        out_shape=pltpu.VMEM((2 * first.shape[0], first.shape[1]), first.dtype),
        cost_estimate=COST,
        compiler_params=params(8),
        name="join",
    )(*in_vmem(first, second))


def finish_kernel(mine, *refs, twins, lows):
    out = refs[-1]
    pieces, low_parts, high_parts = refs[:twins], refs[twins : twins + lows], refs[twins + lows : -1]
    half, piece = low_parts[0].shape[0], pieces[0].shape[0]
    step = min(half, piece)
    for first in range(0, 2 * half, step):
        parts, at = (low_parts, first) if first < half else (high_parts, first - half)
        twin = pieces[first // piece][first % piece : first % piece + step]
        total = mine[first : first + step].astype(jnp.float32) + twin.astype(jnp.float32)
        for part in parts:
            total += part[at : at + step].astype(jnp.float32)
        out[first : first + step] = total.astype(out.dtype)


def finish(mine, twins, low_parts, high_parts):
    parts = [*twins, *low_parts, *high_parts]
    return pl.pallas_call(
        functools.partial(finish_kernel, twins=len(twins), lows=len(low_parts)),
        in_specs=[VMEM_SPEC] * (1 + len(parts)),
        out_specs=VMEM_SPEC,
        out_shape=jax.ShapeDtypeStruct(mine.shape, mine.dtype),
        cost_estimate=COST,
        compiler_params=params(8),
        name="finish",
    )(*in_vmem(mine, *parts))


def on_four_chips(whole, low, high, w_gate, w_up, w_down):
    x, y = 2, 4
    near_x, near_y = flip(low, x), flip(high, y)
    weights = (w_gate, w_up, w_down)
    hidden = hidden_units([whole, flip(whole, CORE)], w_gate, w_up)
    near_x, near_y, hidden = lax.optimization_barrier((near_x, near_y, hidden))
    far_low, far_high = flip(near_x, y), flip(near_y, x)
    parts = [near_x, near_y, flip(near_x, CORE), flip(near_y, CORE)]
    mine_near, other_near = chunk(parts, *weights)
    far_low, far_high, mine_near, low, high = lax.optimization_barrier((far_low, far_high, mine_near, low, high))
    parts = [far_low, far_high, flip(far_low, CORE), flip(far_high, CORE)]
    next_x, next_y = flip(high, x), flip(low, y)
    sum_x, sum_y = add_halves(mine_near, swap(other_near))
    sum_x, sum_y, *parts = lax.optimization_barrier((sum_x, sum_y, *parts))
    back_x, back_y = flip(sum_x, x), flip(sum_y, y)
    mine_far, other_far = chunk(parts, *weights, pieces=2)
    next_x, next_y, mine_far = lax.optimization_barrier((next_x, next_y, mine_far))
    rows = join(next_x, next_y)
    parts = [rows, flip(rows, CORE)]
    relay_low, relay_high = add_halves(mine_far, swap(other_far))
    relay_low, relay_high, *parts = lax.optimization_barrier((relay_low, relay_high, *parts))
    relay_low, relay_high = flip(relay_low, x), flip(relay_high, y)
    mine_next, other_next = chunk(parts, *weights, pieces=2)
    mine_next, hidden, back_x, back_y = lax.optimization_barrier((mine_next, hidden, back_x, back_y))
    mine_own, other_own = down_units(hidden, w_down)
    mine_next, mine_own = lax.optimization_barrier((mine_next, mine_own))
    sum_x, sum_y = add_halves(add_relay(mine_next, relay_high, relay_low), swap(other_next))
    last_x, last_y = flip(sum_x, x), flip(sum_y, y)
    return finish(mine_own, swap(other_own), [back_x, last_y], [back_y, last_x])


def on_any_chips(whole, low, high, *weights):
    offsets = range(2, lax.axis_size("ep"), 2)
    arrived = [flip(whole, d) for d in offsets]
    mine_own, other_own = chunk([whole, flip(whole, CORE)], *weights)
    low_parts, high_parts = [], []
    for d, rows in zip(offsets, arrived):
        mine, others = chunk([rows, flip(rows, CORE)], *weights)
        low, high = add_halves(mine, swap(others))
        low_parts.append(flip(low, d))
        high_parts.append(flip(high, d))
    return finish(mine_own, swap(other_own), low_parts, high_parts)


def body(tokens, experts, gates, w_gate, w_up, w_down):
    n_ep = lax.axis_size("ep")
    n_experts = w_gate.shape[0] * n_ep
    lanes = -(-n_experts // LANES) * LANES
    whole, low, high = prepare(tokens, experts, gates, lanes)
    run = on_four_chips if n_ep == 8 else on_any_chips
    return run(whole, low, high, w_gate, w_up, w_down)


def solution(mesh):
    in_specs = (
        P(("rep", "ep"), None),
        P(("rep", "ep"), None),
        P(("rep", "ep"), None),
        P("ep", None, None),
        P("ep", None, None),
        P("ep", None, None),
    )
    out_specs = P(("rep", "ep"), None)
    return jax.shard_map(body, mesh=mesh, in_specs=in_specs, out_specs=out_specs, check_vma=False)
```

```python
import functools

import jax
import jax.numpy as jnp
from jax import lax
from jax.experimental import pallas as pl
from jax.experimental.pallas import tpu as pltpu
from jax.sharding import PartitionSpec as P

MIB = 2**20
LANES = 128
NT = (((1,), (1,)), ((), ()))
VMEM_SPEC = pl.BlockSpec(memory_space=pltpu.VMEM)
HBM_SPEC = pl.BlockSpec(memory_space=pltpu.HBM)
CORE = 1
LONG = pl.CostEstimate(flops=10**11, bytes_accessed=10**8, transcendentals=0)
COST = pl.CostEstimate(flops=0, bytes_accessed=0, transcendentals=0)


def flip(x, mask):
    n = lax.axis_size("ep")
    return lax.ppermute(x, "ep", [(i, i ^ mask) for i in range(n)])


def cross(x, even, odd):
    n = lax.axis_size("ep")
    return lax.ppermute(x, "ep", [(i, i ^ (odd if i % 2 else even)) for i in range(n)])


def in_vmem(*arrays):
    return [pltpu.with_memory_space_constraint(a, pltpu.VMEM) for a in arrays]


def in_hbm(*arrays):
    return [pltpu.with_memory_space_constraint(a, pltpu.HBM) for a in arrays]


def params(limit=6):
    return pltpu.CompilerParams(vmem_limit_bytes=limit * MIB)


def prepare_kernel(tokens, experts, gates, out, chosen, weight, sems):
    count, width = tokens.shape
    lanes = out.shape[1] - width
    copies = [
        pltpu.make_async_copy(experts, chosen, sems.at[0]),
        pltpu.make_async_copy(gates, weight, sems.at[1]),
        pltpu.make_async_copy(tokens, out.at[:, pl.ds(0, width)], sems.at[2]),
    ]
    for copy in copies:
        copy.start()
    copies[0].wait()
    copies[1].wait()
    ids = lax.broadcasted_iota(jnp.int32, (lanes, count), 0)
    total = jnp.zeros((lanes, count), jnp.float32)
    for k in range(chosen.shape[0]):
        gate = weight[k : k + 1, :].astype(jnp.float32)
        total += jnp.where(ids == chosen[k : k + 1, :], gate, 0.0)
    out[:, width:] = total.T.astype(jnp.bfloat16)
    copies[2].wait()


def prepare(tokens, experts, gates, lanes):
    count, width = tokens.shape
    return pl.pallas_call(
        prepare_kernel,
        in_specs=[HBM_SPEC] * 3,
        out_specs=VMEM_SPEC,
        out_shape=pltpu.VMEM((count, width + lanes), jnp.bfloat16),
        scratch_shapes=[
            pltpu.VMEM(experts.shape[::-1], jnp.int32),
            pltpu.VMEM(gates.shape[::-1], jnp.bfloat16),
            pltpu.SemaphoreType.DMA((3,)),
        ],
        cost_estimate=LONG,
        compiler_params=params(4),
        name="prepare",
    )(*in_hbm(tokens, experts.T, gates.T))


def gather_inputs(parts, rows, held):
    width = rows.shape[1]
    tables, start = [], 0
    for part in parts:
        rows[start : start + part.shape[0]] = part[:, :width]
        tables.append(part[:, width:])
        start += part.shape[0]
    table = jnp.concatenate(tables, axis=0).astype(jnp.float32)
    lane = lax.broadcasted_iota(jnp.int32, table.shape, 1)
    base = lax.axis_index("ep") * held
    return [
        jnp.sum(jnp.where(lane == base + e, table, 0.0), axis=1, keepdims=True) for e in range(held)
    ]


def gated_of(rows, gate_w, weight):
    gate_act = jnp.dot(rows, gate_w, preferred_element_type=jnp.float32)
    return gate_act / (1.0 + jnp.exp(-gate_act)) * weight


def hidden_of(rows, gate_w, up_w, weight):
    up_act = jnp.dot(rows, up_w, preferred_element_type=jnp.float32)
    return (gated_of(rows, gate_w, weight) * up_act).astype(jnp.bfloat16)


def down_all(hidden, w_down, mine, other, tile=512):
    held, width, units = w_down.shape
    count = mine.shape[0]
    for start in range(0, width, tile):
        total = None
        for e in range(held):
            part = lax.dot_general(
                hidden[:, e * units : (e + 1) * units],
                w_down[e, start : start + tile, :],
                NT,
                preferred_element_type=jnp.float32,
            )
            total = part if total is None else total + part
        total = total.astype(jnp.bfloat16)
        mine[:, start : start + tile] = total[:count]
        other[:, start : start + tile] = total[count:]


def gated_kernel(*refs, parts):
    inputs, (w_gate, gated, rows) = refs[:parts], refs[parts:]
    held, _, units = w_gate.shape
    weights = gather_inputs(inputs, rows, held)
    for e in range(held):
        gated[:, e * units : (e + 1) * units] = gated_of(rows[...], w_gate[e], weights[e])


def gated_units(parts, w_gate):
    count = sum(part.shape[0] for part in parts)
    held, width, units = w_gate.shape
    return pl.pallas_call(
        functools.partial(gated_kernel, parts=len(parts)),
        in_specs=[VMEM_SPEC] * (len(parts) + 1),
        out_specs=[VMEM_SPEC] * 2,
        out_shape=[pltpu.VMEM((count, held * units), jnp.float32), pltpu.VMEM((count, width), jnp.bfloat16)],
        cost_estimate=COST,
        compiler_params=params(),
        name="gated_units",
    )(*in_vmem(*parts, w_gate))


def hidden_kernel(gated, rows, w_up, hidden):
    held, _, units = w_up.shape
    for e in range(held):
        block = slice(e * units, (e + 1) * units)
        up_act = jnp.dot(rows[...], w_up[e], preferred_element_type=jnp.float32)
        hidden[:, block] = (gated[:, block] * up_act).astype(jnp.bfloat16)


def hidden_units(gated, rows, w_up):
    return pl.pallas_call(
        hidden_kernel,
        in_specs=[VMEM_SPEC] * 3,
        out_specs=VMEM_SPEC,
        out_shape=pltpu.VMEM(gated.shape, jnp.bfloat16),
        cost_estimate=COST,
        compiler_params=params(),
        name="hidden_units",
    )(*in_vmem(gated, rows, w_up))


def units_kernel(*refs, parts):
    inputs, (w_gate, w_up, hidden, rows) = refs[:parts], refs[parts:]
    held, _, units = w_gate.shape
    weights = gather_inputs(inputs, rows, held)
    for e in range(held):
        hidden[:, e * units : (e + 1) * units] = hidden_of(rows[...], w_gate[e], w_up[e], weights[e])


def units_of(parts, w_gate, w_up):
    count = sum(part.shape[0] for part in parts)
    held, width, units = w_gate.shape
    return pl.pallas_call(
        functools.partial(units_kernel, parts=len(parts)),
        in_specs=[VMEM_SPEC] * (len(parts) + 2),
        out_specs=VMEM_SPEC,
        out_shape=pltpu.VMEM((count, held * units), jnp.bfloat16),
        scratch_shapes=[pltpu.VMEM((count, width), jnp.bfloat16)],
        cost_estimate=COST,
        compiler_params=params(),
        name="units_of",
    )(*in_vmem(*parts, w_gate, w_up))


def rest_kernel(first, part, w_gate, w_up, w_down, mine, other, rows, hidden):
    held, _, units = w_gate.shape
    count = first.shape[0]
    weights = gather_inputs([part], rows, held)
    for e in range(held):
        block = slice(e * units, (e + 1) * units)
        hidden[:count, block] = first[:, block]
        hidden[count:, block] = hidden_of(rows[...], w_gate[e], w_up[e], weights[e])
    down_all(hidden, w_down, mine, other)


def rest_of(first, part, w_gate, w_up, w_down):
    count = part.shape[0]
    held, width, units = w_gate.shape
    return pl.pallas_call(
        rest_kernel,
        in_specs=[VMEM_SPEC] * 5,
        out_specs=[VMEM_SPEC] * 2,
        out_shape=[pltpu.VMEM((count, width), jnp.bfloat16)] * 2,
        scratch_shapes=[
            pltpu.VMEM((count, width), jnp.bfloat16),
            pltpu.VMEM((2 * count, held * units), jnp.bfloat16),
        ],
        cost_estimate=COST,
        compiler_params=params(),
        name="rest_of",
    )(*in_vmem(first, part, w_gate, w_up, w_down))


def down_units(hidden, w_down):
    half = pltpu.VMEM((hidden.shape[0] // 2, w_down.shape[1]), jnp.bfloat16)
    return pl.pallas_call(
        down_all,
        in_specs=[VMEM_SPEC] * 2,
        out_specs=[VMEM_SPEC] * 2,
        out_shape=[half, half],
        cost_estimate=COST,
        compiler_params=params(),
        name="down_units",
    )(*in_vmem(hidden, w_down))


def add_kernel(*refs):
    *parts, out = refs
    width = parts[0].shape[1]
    total = parts[0][...].astype(jnp.float32)
    for part in parts[1:]:
        total += part[:, :width].astype(jnp.float32)
    out[:, :width] = total.astype(out.dtype)
    if out.shape[1] > width:
        out[:, width:] = jnp.zeros((out.shape[0], out.shape[1] - width), out.dtype)


def add(*parts, dtype=jnp.bfloat16, spare=0, cost=COST):
    count, width = parts[0].shape
    return pl.pallas_call(
        add_kernel,
        in_specs=[VMEM_SPEC] * len(parts),
        out_specs=VMEM_SPEC,
        out_shape=pltpu.VMEM((count, width + spare), dtype),
        cost_estimate=cost,
        compiler_params=params(8),
        name="add",
    )(*in_vmem(*parts))


def finish(*parts):
    count, width = parts[0].shape
    return pl.pallas_call(
        add_kernel,
        in_specs=[VMEM_SPEC] * len(parts),
        out_specs=VMEM_SPEC,
        out_shape=jax.ShapeDtypeStruct((count, width), jnp.bfloat16),
        cost_estimate=COST,
        compiler_params=params(8),
        name="finish",
    )(*in_vmem(*parts))


def on_four_chips(own, w_gate, w_up, w_down):
    x, y = 2, 4
    barrier = lax.optimization_barrier
    weights = (w_gate, w_up, w_down)
    near = cross(own, x, y)
    hidden = hidden_units(*gated_units([own, flip(own, CORE)], w_gate), w_up)
    near, hidden = barrier((near, hidden))

    far = cross(near, y, x)
    mine_near, other_near = rest_of(units_of([near], w_gate, w_up), flip(near, CORE), *weights)
    far, own, mine_near = barrier((far, own, mine_near))

    following = cross(own, y, x)
    far_twin = flip(far, CORE)
    sum_near = add(mine_near, flip(other_near, CORE), spare=2 * LANES, cost=LONG)
    sum_near, far_twin = barrier((sum_near, far_twin))
    units = units_of([far, far_twin], w_gate, w_up)
    sum_near, units = barrier((sum_near, units))
    back = cross(sum_near, x, y)
    mine_far, other_far = down_units(units, w_down)
    following, mine_far = barrier((following, mine_far))

    following_twin = flip(following, CORE)
    first = units_of([following], w_gate, w_up)
    mine_far, first = barrier((mine_far, first))
    sum_far = add(mine_far, flip(other_far, CORE))
    sum_far, following_twin, first = barrier((sum_far, following_twin, first))
    relay = cross(sum_far, x, y)
    first, back = barrier((first, back))
    mine_last, other_last = rest_of(first, following_twin, *weights)
    mine_last, hidden = barrier((mine_last, hidden))

    mine_own, other_own = down_units(hidden, w_down)
    mine_last, mine_own = barrier((mine_last, mine_own))
    sum_last = add(add(mine_last, relay, dtype=jnp.float32), flip(other_last, CORE))
    last = cross(sum_last, y, x)
    return finish(mine_own, flip(other_own, CORE), back, last)


def on_any_chips(own, *weights):
    offsets = range(2, lax.axis_size("ep"), 2)
    arrived = [flip(own, d) for d in offsets]
    parts = []
    for d, rows in zip([0, *offsets], [own, *arrived]):
        mine, other = rest_of(units_of([rows], *weights[:2]), flip(rows, CORE), *weights)
        other = flip(other, CORE)
        parts += [flip(add(mine, other), d)] if d else [mine, other]
    return finish(*parts)


def body(tokens, experts, gates, w_gate, w_up, w_down):
    n_ep = lax.axis_size("ep")
    n_experts = w_gate.shape[0] * n_ep
    lanes = -(-n_experts // LANES) * LANES
    own = prepare(tokens, experts, gates, lanes)
    run = on_four_chips if n_ep == 8 else on_any_chips
    return run(own, w_gate, w_up, w_down)


def solution(mesh):
    in_specs = (
        P(("rep", "ep"), None),
        P(("rep", "ep"), None),
        P(("rep", "ep"), None),
        P("ep", None, None),
        P("ep", None, None),
        P("ep", None, None),
    )
    out_specs = P(("rep", "ep"), None)
    return jax.shard_map(body, mesh=mesh, in_specs=in_specs, out_specs=out_specs, check_vma=False)
```

```python
import functools

import jax
import jax.numpy as jnp
from jax import lax
from jax.experimental import pallas as pl
from jax.experimental.pallas import tpu as pltpu
from jax.sharding import PartitionSpec as P

MIB = 2**20
LANES = 128
NT = (((1,), (1,)), ((), ()))
VMEM_SPEC = pl.BlockSpec(memory_space=pltpu.VMEM)
HBM_SPEC = pl.BlockSpec(memory_space=pltpu.HBM)
CORE = 1
MEDIUM = pl.CostEstimate(flops=0, bytes_accessed=3 * 10**6, transcendentals=0)
RELAY = pl.CostEstimate(flops=2 * 10**9, bytes_accessed=3 * 10**6, transcendentals=0)
LONG = pl.CostEstimate(flops=10**11, bytes_accessed=10**8, transcendentals=0)
COST = pl.CostEstimate(flops=0, bytes_accessed=0, transcendentals=0)


def flip(x, mask):
    n = lax.axis_size("ep")
    return lax.ppermute(x, "ep", [(i, i ^ mask) for i in range(n)])


def cross(x, even, odd):
    n = lax.axis_size("ep")
    return lax.ppermute(x, "ep", [(i, i ^ (odd if i % 2 else even)) for i in range(n)])


def in_vmem(*arrays):
    return [pltpu.with_memory_space_constraint(a, pltpu.VMEM) for a in arrays]


def in_hbm(*arrays):
    return [pltpu.with_memory_space_constraint(a, pltpu.HBM) for a in arrays]


def params(limit=6):
    return pltpu.CompilerParams(vmem_limit_bytes=limit * MIB)


def prepare_kernel(tokens, experts, gates, out, wide, chosen, weight, sems):
    count, width = tokens.shape
    lanes = out.shape[1] - width
    copies = [
        pltpu.make_async_copy(experts, chosen, sems.at[0]),
        pltpu.make_async_copy(gates, weight, sems.at[1]),
        pltpu.make_async_copy(tokens, out.at[:, pl.ds(0, width)], sems.at[2]),
        pltpu.make_async_copy(tokens, wide.at[:, pl.ds(0, width)], sems.at[3]),
    ]
    for copy in copies:
        copy.start()
    copies[0].wait()
    copies[1].wait()
    ids = lax.broadcasted_iota(jnp.int32, (lanes, count), 0)
    total = jnp.zeros((lanes, count), jnp.float32)
    for k in range(chosen.shape[0]):
        gate = weight[k : k + 1, :].astype(jnp.float32)
        total += jnp.where(ids == chosen[k : k + 1, :], gate, 0.0)
    table = total.T.astype(jnp.bfloat16)
    out[:, width:] = table
    wide[:, width : width + lanes] = table
    wide[:, width + lanes :] = jnp.zeros((count, wide.shape[1] - width - lanes), jnp.bfloat16)
    copies[2].wait()
    copies[3].wait()


def prepare(tokens, experts, gates, lanes):
    count, width = tokens.shape
    return pl.pallas_call(
        prepare_kernel,
        in_specs=[HBM_SPEC] * 3,
        out_specs=[VMEM_SPEC] * 2,
        out_shape=[pltpu.VMEM((count, width + lanes + spare), jnp.bfloat16) for spare in (0, LANES)],
        scratch_shapes=[
            pltpu.VMEM(experts.shape[::-1], jnp.int32),
            pltpu.VMEM(gates.shape[::-1], jnp.bfloat16),
            pltpu.SemaphoreType.DMA((4,)),
        ],
        cost_estimate=LONG,
        compiler_params=params(4),
        name="prepare",
    )(*in_hbm(tokens, experts.T, gates.T))


def gather_inputs(parts, rows, held):
    width = rows.shape[1]
    tables, start = [], 0
    for part in parts:
        rows[start : start + part.shape[0]] = part[:, :width]
        tables.append(part[:, width:])
        start += part.shape[0]
    table = jnp.concatenate(tables, axis=0).astype(jnp.float32)
    lane = lax.broadcasted_iota(jnp.int32, table.shape, 1)
    base = lax.axis_index("ep") * held
    return [
        jnp.sum(jnp.where(lane == base + e, table, 0.0), axis=1, keepdims=True) for e in range(held)
    ]


def gated_of(rows, gate_w, weight):
    gate_act = jnp.dot(rows, gate_w, preferred_element_type=jnp.float32)
    return gate_act / (1.0 + jnp.exp(-gate_act)) * weight


def hidden_of(rows, gate_w, up_w, weight):
    up_act = jnp.dot(rows, up_w, preferred_element_type=jnp.float32)
    return (gated_of(rows, gate_w, weight) * up_act).astype(jnp.bfloat16)


def down_all(hidden, w_down, mine, *others, tile=512):
    held, width, units = w_down.shape
    count, piece = mine.shape[0], others[0].shape[0]
    for start in range(0, width, tile):
        total = None
        for e in range(held):
            part = lax.dot_general(
                hidden[:, e * units : (e + 1) * units],
                w_down[e, start : start + tile, :],
                NT,
                preferred_element_type=jnp.float32,
            )
            total = part if total is None else total + part
        total = total.astype(jnp.bfloat16)
        mine[:, start : start + tile] = total[:count]
        for i, other in enumerate(others):
            row = count + i * piece
            other[:, start : start + tile] = total[row : row + piece]


def gated_kernel(*refs, parts):
    inputs, (w_gate, gated, rows) = refs[:parts], refs[parts:]
    held, _, units = w_gate.shape
    weights = gather_inputs(inputs, rows, held)
    for e in range(held):
        gated[:, e * units : (e + 1) * units] = gated_of(rows[...], w_gate[e], weights[e])


def gated_units(parts, w_gate):
    count = sum(part.shape[0] for part in parts)
    held, width, units = w_gate.shape
    return pl.pallas_call(
        functools.partial(gated_kernel, parts=len(parts)),
        in_specs=[VMEM_SPEC] * (len(parts) + 1),
        out_specs=[VMEM_SPEC] * 2,
        out_shape=[pltpu.VMEM((count, held * units), jnp.float32), pltpu.VMEM((count, width), jnp.bfloat16)],
        cost_estimate=COST,
        compiler_params=params(),
        name="gated_units",
    )(*in_vmem(*parts, w_gate))


def hidden_kernel(gated, rows, w_up, hidden):
    held, _, units = w_up.shape
    for e in range(held):
        block = slice(e * units, (e + 1) * units)
        up_act = jnp.dot(rows[...], w_up[e], preferred_element_type=jnp.float32)
        hidden[:, block] = (gated[:, block] * up_act).astype(jnp.bfloat16)


def hidden_units(gated, rows, w_up):
    return pl.pallas_call(
        hidden_kernel,
        in_specs=[VMEM_SPEC] * 3,
        out_specs=VMEM_SPEC,
        out_shape=pltpu.VMEM(gated.shape, jnp.bfloat16),
        cost_estimate=COST,
        compiler_params=params(),
        name="hidden_units",
    )(*in_vmem(gated, rows, w_up))


def units_kernel(*refs, parts):
    inputs, (w_gate, w_up), (hidden, rows) = refs[:parts], refs[parts : parts + 2], refs[-2:]
    held, _, units = w_gate.shape
    weights = gather_inputs(inputs, rows, held)
    for e in range(held):
        hidden[:, e * units : (e + 1) * units] = hidden_of(rows[...], w_gate[e], w_up[e], weights[e])


def units_of(parts, w_gate, w_up, *others):
    count = sum(part.shape[0] for part in parts)
    held, width, units = w_gate.shape
    return pl.pallas_call(
        functools.partial(units_kernel, parts=len(parts)),
        in_specs=[VMEM_SPEC] * (len(parts) + 2 + len(others)),
        out_specs=VMEM_SPEC,
        out_shape=pltpu.VMEM((count, held * units), jnp.bfloat16),
        scratch_shapes=[pltpu.VMEM((count, width), jnp.bfloat16)],
        cost_estimate=COST,
        compiler_params=params(),
        name="units_of",
    )(*in_vmem(*parts, w_gate, w_up, *others))


def rest_kernel(first, part, w_gate, w_up, w_down, mine, other, rows, hidden):
    held, _, units = w_gate.shape
    count = first.shape[0]
    weights = gather_inputs([part], rows, held)
    for e in range(held):
        block = slice(e * units, (e + 1) * units)
        hidden[:count, block] = first[:, block]
        hidden[count:, block] = hidden_of(rows[...], w_gate[e], w_up[e], weights[e])
    down_all(hidden, w_down, mine, other)


def rest_of(first, part, w_gate, w_up, w_down):
    count = part.shape[0]
    held, width, units = w_gate.shape
    return pl.pallas_call(
        rest_kernel,
        in_specs=[VMEM_SPEC] * 5,
        out_specs=[VMEM_SPEC] * 2,
        out_shape=[pltpu.VMEM((count, width), jnp.bfloat16)] * 2,
        scratch_shapes=[
            pltpu.VMEM((count, width), jnp.bfloat16),
            pltpu.VMEM((2 * count, held * units), jnp.bfloat16),
        ],
        cost_estimate=COST,
        compiler_params=params(),
        name="rest_of",
    )(*in_vmem(first, part, w_gate, w_up, w_down))


def sums_kernel(first, second, w_down, mine, *refs):
    *others, hidden = refs
    count = first.shape[0]
    hidden[:count] = first[...]
    hidden[count:] = second[...]
    down_all(hidden, w_down, mine, *others)


def sums_of(first, second, w_down, pieces=1):
    count, width = first.shape[0], w_down.shape[1]
    others = [pltpu.VMEM((count // pieces, width), jnp.bfloat16)] * pieces
    return pl.pallas_call(
        sums_kernel,
        in_specs=[VMEM_SPEC] * 3,
        out_specs=[VMEM_SPEC] * (1 + pieces),
        out_shape=[pltpu.VMEM((count, width), jnp.bfloat16), *others],
        scratch_shapes=[pltpu.VMEM((2 * count, first.shape[1]), jnp.bfloat16)],
        cost_estimate=COST,
        compiler_params=params(),
        name="sums_of",
    )(*in_vmem(first, second, w_down))


def join_kernel(mine, *refs):
    *others, out = refs
    piece = others[0].shape[0]
    for i, other in enumerate(others):
        rows = slice(i * piece, (i + 1) * piece)
        out[rows] = (mine[rows].astype(jnp.float32) + other[...].astype(jnp.float32)).astype(out.dtype)


def add_pieces(mine, others):
    return pl.pallas_call(
        join_kernel,
        in_specs=[VMEM_SPEC] * (1 + len(others)),
        out_specs=VMEM_SPEC,
        out_shape=pltpu.VMEM(mine.shape, mine.dtype),
        cost_estimate=COST,
        compiler_params=params(8),
        name="add_pieces",
    )(*in_vmem(mine, *others))


def down_units(hidden, w_down):
    half = pltpu.VMEM((hidden.shape[0] // 2, w_down.shape[1]), jnp.bfloat16)
    return pl.pallas_call(
        down_all,
        in_specs=[VMEM_SPEC] * 2,
        out_specs=[VMEM_SPEC] * 2,
        out_shape=[half, half],
        cost_estimate=COST,
        compiler_params=params(),
        name="down_units",
    )(*in_vmem(hidden, w_down))


def add_kernel(*refs):
    *parts, out = refs
    width = parts[0].shape[1]
    total = parts[0][...].astype(jnp.float32)
    for part in parts[1:]:
        total += part[:, :width].astype(jnp.float32)
    out[:, :width] = total.astype(out.dtype)
    if out.shape[1] > width:
        out[:, width:] = jnp.zeros((out.shape[0], out.shape[1] - width), out.dtype)


def add(*parts, dtype=jnp.bfloat16, spare=0, cost=COST):
    count, width = parts[0].shape
    return pl.pallas_call(
        add_kernel,
        in_specs=[VMEM_SPEC] * len(parts),
        out_specs=VMEM_SPEC,
        out_shape=pltpu.VMEM((count, width + spare), dtype),
        cost_estimate=cost,
        compiler_params=params(8),
        name="add",
    )(*in_vmem(*parts))


def trim_kernel(rows, out):
    out[...] = rows[:, : out.shape[1]]


def trim(rows, columns):
    return pl.pallas_call(
        trim_kernel,
        in_specs=[VMEM_SPEC],
        out_specs=VMEM_SPEC,
        out_shape=pltpu.VMEM((rows.shape[0], columns), rows.dtype),
        cost_estimate=COST,
        compiler_params=params(8),
        name="trim",
    )(*in_vmem(rows))


def finish(*parts):
    count, width = parts[0].shape
    return pl.pallas_call(
        add_kernel,
        in_specs=[VMEM_SPEC] * len(parts),
        out_specs=VMEM_SPEC,
        out_shape=jax.ShapeDtypeStruct((count, width), jnp.bfloat16),
        cost_estimate=COST,
        compiler_params=params(8),
        name="finish",
    )(*in_vmem(*parts))


def on_four_chips(own, wide, w_gate, w_up, w_down):
    x, y = 2, 4
    barrier = lax.optimization_barrier
    weights = (w_gate, w_up, w_down)
    near = cross(own, x, y)
    hidden = hidden_units(*gated_units([own, flip(own, CORE)], w_gate), w_up)
    near, hidden = barrier((near, hidden))

    far = cross(near, y, x)
    mine_near, other_near = rest_of(units_of([near], *weights), flip(near, CORE), *weights)
    following = cross(wide, y, x)
    far, mine_near = barrier((far, mine_near))

    far_twin = flip(far, CORE)
    first = units_of([far], w_gate, w_up)
    first, far_twin = barrier((first, far_twin))
    second = units_of([far_twin], w_gate, w_up)
    mine_near, second = barrier((mine_near, second))
    sum_near = add(mine_near, flip(other_near, CORE))
    back = cross(sum_near, x, y)
    following, second = barrier((following, second))
    mine_far, *other_far = sums_of(first, second, w_down, pieces=2)

    following = trim(following, own.shape[1])
    following_twin = flip(following, CORE)
    first = units_of([following], w_gate, w_up)
    mine_far, first = barrier((mine_far, first))
    sum_far = add_pieces(mine_far, [flip(other, CORE) for other in other_far])
    sum_far, following_twin, first = barrier((sum_far, following_twin, first))
    relay = cross(sum_far, x, y)
    second = units_of([following_twin], w_gate, w_up)
    second, back = barrier((second, back))
    mine_last, other_last = sums_of(first, second, w_down)
    mine_last, hidden = barrier((mine_last, hidden))
    mine_own, other_own = down_units(hidden, w_down)
    mine_last, mine_own = barrier((mine_last, mine_own))
    sum_last = add(add(mine_last, relay, dtype=jnp.float32, cost=RELAY), flip(other_last, CORE))
    last = cross(sum_last, y, x)
    return finish(mine_own, flip(other_own, CORE), back, last)


def on_any_chips(own, _, *weights):
    offsets = range(2, lax.axis_size("ep"), 2)
    arrived = [flip(own, d) for d in offsets]
    parts = []
    for d, rows in zip([0, *offsets], [own, *arrived]):
        mine, other = rest_of(units_of([rows], *weights[:2]), flip(rows, CORE), *weights)
        other = flip(other, CORE)
        parts += [flip(add(mine, other), d)] if d else [mine, other]
    return finish(*parts)


def body(tokens, experts, gates, w_gate, w_up, w_down):
    n_ep = lax.axis_size("ep")
    n_experts = w_gate.shape[0] * n_ep
    lanes = -(-n_experts // LANES) * LANES
    own, wide = prepare(tokens, experts, gates, lanes)
    run = on_four_chips if n_ep == 8 else on_any_chips
    return run(own, wide, w_gate, w_up, w_down)


def solution(mesh):
    in_specs = (
        P(("rep", "ep"), None),
        P(("rep", "ep"), None),
        P(("rep", "ep"), None),
        P("ep", None, None),
        P("ep", None, None),
        P("ep", None, None),
    )
    out_specs = P(("rep", "ep"), None)
    return jax.shard_map(body, mesh=mesh, in_specs=in_specs, out_specs=out_specs, check_vma=False)
```

```python
import functools

import jax
import jax.numpy as jnp
from jax import lax
from jax.experimental import pallas as pl
from jax.experimental.pallas import tpu as pltpu
from jax.sharding import PartitionSpec as P

MIB = 2**20
LANES = 128
NT = (((1,), (1,)), ((), ()))
VMEM_SPEC = pl.BlockSpec(memory_space=pltpu.VMEM)
HBM_SPEC = pl.BlockSpec(memory_space=pltpu.HBM)
CORE = 1
PACK = 16
SPARE = 4 * LANES
MEDIUM = pl.CostEstimate(flops=0, bytes_accessed=3 * 10**6, transcendentals=0)
RELAY = pl.CostEstimate(flops=2 * 10**9, bytes_accessed=3 * 10**6, transcendentals=0)
LONG = pl.CostEstimate(flops=10**11, bytes_accessed=10**8, transcendentals=0)
COST = pl.CostEstimate(flops=0, bytes_accessed=0, transcendentals=0)


def flip(x, mask):
    n = lax.axis_size("ep")
    return lax.ppermute(x, "ep", [(i, i ^ mask) for i in range(n)])


def cross(x, even, odd):
    n = lax.axis_size("ep")
    return lax.ppermute(x, "ep", [(i, i ^ (odd if i % 2 else even)) for i in range(n)])


def in_vmem(*arrays):
    return [pltpu.with_memory_space_constraint(a, pltpu.VMEM) for a in arrays]


def in_hbm(*arrays):
    return [pltpu.with_memory_space_constraint(a, pltpu.HBM) for a in arrays]


def params(limit=6):
    return pltpu.CompilerParams(vmem_limit_bytes=limit * MIB)


def prepare_kernel(tokens, experts, gates, low, high, table, chosen, weight, sems, *, n_experts):
    count, width = tokens.shape
    groups = count // PACK
    half = groups // 2
    copies = [
        pltpu.make_async_copy(experts, chosen, sems.at[0]),
        pltpu.make_async_copy(gates, weight, sems.at[1]),
    ]
    for j in range(groups):
        rows = tokens.at[pl.ds(j * PACK, PACK)]
        place = (low if j < half else high).at[:, pl.ds(j % half * width, width)]
        copies.append(pltpu.make_async_copy(rows, place, sems.at[2 + j]))
    for copy in copies:
        copy.start()
    copies[0].wait()
    copies[1].wait()
    ids = lax.broadcasted_iota(jnp.int32, (-(-n_experts // LANES) * LANES, count), 0)
    total = jnp.zeros(ids.shape, jnp.float32)
    for k in range(chosen.shape[0]):
        gate = weight[k : k + 1, :].astype(jnp.float32)
        total += jnp.where(ids == chosen[k : k + 1, :], gate, 0.0)
    total = total.T
    blocks = [total[j * PACK : (j + 1) * PACK, :n_experts] for j in range(groups)]
    for out, first, last in ((low, 0, half), (high, half, groups), (table, 0, groups)):
        start = 0 if out is table else half * width
        spare = out.shape[1] - start - (last - first) * n_experts
        values = blocks[first:last] + ([jnp.zeros((PACK, spare), jnp.float32)] if spare else [])
        out[:, start:] = jnp.concatenate(values, axis=1).astype(jnp.bfloat16)
    for copy in copies[2:]:
        copy.wait()


def table_lanes(groups, n_experts):
    return -(-groups * n_experts // LANES) * LANES


def prepare(tokens, experts, gates, n_experts):
    count, width = tokens.shape
    groups = count // PACK
    half = groups // 2 * width + table_lanes(groups // 2, n_experts)
    lanes = [half, half, table_lanes(groups, n_experts)]
    return pl.pallas_call(
        functools.partial(prepare_kernel, n_experts=n_experts),
        in_specs=[HBM_SPEC] * 3,
        out_specs=[VMEM_SPEC] * 3,
        out_shape=[pltpu.VMEM((PACK, size), jnp.bfloat16) for size in lanes],
        scratch_shapes=[
            pltpu.VMEM(experts.shape[::-1], jnp.int32),
            pltpu.VMEM(gates.shape[::-1], jnp.bfloat16),
            pltpu.SemaphoreType.DMA((2 + groups,)),
        ],
        cost_estimate=LONG,
        compiler_params=params(4),
        name="prepare",
    )(*in_hbm(tokens, experts.T, gates.T))


def join_kernel(low, high, table, out, *, width):
    part = low.shape[1] // width * width
    out[:, :part] = low[:, :part]
    out[:, part : 2 * part] = high[:, :part]
    out[:, 2 * part : 2 * part + table.shape[1]] = table[...]
    if out.shape[1] > 2 * part + table.shape[1]:
        spare = out.shape[1] - 2 * part - table.shape[1]
        out[:, 2 * part + table.shape[1] :] = jnp.zeros((PACK, spare), out.dtype)


def join(low, high, table, width, spare=0):
    lanes = low.shape[1] // width * width * 2 + table.shape[1] + spare
    return pl.pallas_call(
        functools.partial(join_kernel, width=width),
        in_specs=[VMEM_SPEC] * 3,
        out_specs=VMEM_SPEC,
        out_shape=pltpu.VMEM((PACK, lanes), low.dtype),
        cost_estimate=COST,
        compiler_params=params(4),
        name="join",
    )(*in_vmem(low, high, table))


def pack_kernel(rows, table, out):
    width = rows.shape[1]
    for j in range(rows.shape[0] // PACK):
        out[:, j * width : (j + 1) * width] = rows[j * PACK : (j + 1) * PACK]
    out[:, rows.shape[0] // PACK * width :] = table[...]


def pack(rows, table):
    return pl.pallas_call(
        pack_kernel,
        in_specs=[VMEM_SPEC] * 2,
        out_specs=VMEM_SPEC,
        out_shape=pltpu.VMEM((PACK, rows.size // PACK + table.shape[1]), rows.dtype),
        cost_estimate=COST,
        compiler_params=params(4),
        name="pack",
    )(*in_vmem(rows, table))


def rows_in(part, width):
    return part.shape[1] // width * PACK


def gather_inputs(parts, rows, held):
    width = rows.shape[1]
    n_experts = held * lax.axis_size("ep")
    base = lax.axis_index("ep") * held
    columns = [[] for _ in range(held)]
    start = 0
    for part in parts:
        groups = part.shape[1] // width
        table = part[:, groups * width :].astype(jnp.float32)
        lane = lax.broadcasted_iota(jnp.int32, table.shape, 1)
        for j in range(groups):
            rows[start : start + PACK] = part[:, j * width : (j + 1) * width]
            start += PACK
            for e in range(held):
                gate = jnp.where(lane == j * n_experts + base + e, table, 0.0)
                columns[e].append(jnp.sum(gate, axis=1, keepdims=True))
    return [jnp.concatenate(column, axis=0) for column in columns]


def gated_of(rows, gate_w, weight):
    gate_act = jnp.dot(rows, gate_w, preferred_element_type=jnp.float32)
    return gate_act / (1.0 + jnp.exp(-gate_act)) * weight


def hidden_of(rows, gate_w, up_w, weight):
    up_act = jnp.dot(rows, up_w, preferred_element_type=jnp.float32)
    return (gated_of(rows, gate_w, weight) * up_act).astype(jnp.bfloat16)


def down_all(hidden, w_down, mine, *others, tile=512):
    held, width, units = w_down.shape
    count, piece = mine.shape[0], others[0].shape[0]
    for start in range(0, width, tile):
        total = None
        for e in range(held):
            part = lax.dot_general(
                hidden[:, e * units : (e + 1) * units],
                w_down[e, start : start + tile, :],
                NT,
                preferred_element_type=jnp.float32,
            )
            total = part if total is None else total + part
        total = total.astype(jnp.bfloat16)
        mine[:, start : start + tile] = total[:count]
        for i, other in enumerate(others):
            row = count + i * piece
            other[:, start : start + tile] = total[row : row + piece]


def gated_kernel(*refs, parts):
    inputs, (w_gate, gated, rows) = refs[:parts], refs[parts:]
    held, _, units = w_gate.shape
    weights = gather_inputs(inputs, rows, held)
    for e in range(held):
        gated[:, e * units : (e + 1) * units] = gated_of(rows[...], w_gate[e], weights[e])


def gated_units(parts, w_gate):
    held, width, units = w_gate.shape
    count = sum(rows_in(part, width) for part in parts)
    return pl.pallas_call(
        functools.partial(gated_kernel, parts=len(parts)),
        in_specs=[VMEM_SPEC] * (len(parts) + 1),
        out_specs=[VMEM_SPEC] * 2,
        out_shape=[pltpu.VMEM((count, held * units), jnp.float32), pltpu.VMEM((count, width), jnp.bfloat16)],
        cost_estimate=COST,
        compiler_params=params(),
        name="gated_units",
    )(*in_vmem(*parts, w_gate))


def hidden_kernel(gated, rows, w_up, hidden):
    held, _, units = w_up.shape
    for e in range(held):
        block = slice(e * units, (e + 1) * units)
        up_act = jnp.dot(rows[...], w_up[e], preferred_element_type=jnp.float32)
        hidden[:, block] = (gated[:, block] * up_act).astype(jnp.bfloat16)


def hidden_units(gated, rows, w_up):
    return pl.pallas_call(
        hidden_kernel,
        in_specs=[VMEM_SPEC] * 3,
        out_specs=VMEM_SPEC,
        out_shape=pltpu.VMEM(gated.shape, jnp.bfloat16),
        cost_estimate=COST,
        compiler_params=params(),
        name="hidden_units",
    )(*in_vmem(gated, rows, w_up))


def units_kernel(*refs, parts):
    inputs, (w_gate, w_up), (hidden, rows) = refs[:parts], refs[parts : parts + 2], refs[-2:]
    held, _, units = w_gate.shape
    weights = gather_inputs(inputs, rows, held)
    for e in range(held):
        hidden[:, e * units : (e + 1) * units] = hidden_of(rows[...], w_gate[e], w_up[e], weights[e])


def units_of(parts, w_gate, w_up, *others):
    held, width, units = w_gate.shape
    count = sum(rows_in(part, width) for part in parts)
    return pl.pallas_call(
        functools.partial(units_kernel, parts=len(parts)),
        in_specs=[VMEM_SPEC] * (len(parts) + 2 + len(others)),
        out_specs=VMEM_SPEC,
        out_shape=pltpu.VMEM((count, held * units), jnp.bfloat16),
        scratch_shapes=[pltpu.VMEM((count, width), jnp.bfloat16)],
        cost_estimate=COST,
        compiler_params=params(),
        name="units_of",
    )(*in_vmem(*parts, w_gate, w_up, *others))


def rest_kernel(first, part, w_gate, w_up, w_down, mine, other, rows, hidden):
    held, _, units = w_gate.shape
    count = first.shape[0]
    weights = gather_inputs([part], rows, held)
    for e in range(held):
        block = slice(e * units, (e + 1) * units)
        hidden[:count, block] = first[:, block]
        hidden[count:, block] = hidden_of(rows[...], w_gate[e], w_up[e], weights[e])
    down_all(hidden, w_down, mine, other)


def rest_of(first, part, w_gate, w_up, w_down):
    held, width, units = w_gate.shape
    count = rows_in(part, width)
    return pl.pallas_call(
        rest_kernel,
        in_specs=[VMEM_SPEC] * 5,
        out_specs=[VMEM_SPEC] * 2,
        out_shape=[pltpu.VMEM((count, width), jnp.bfloat16)] * 2,
        scratch_shapes=[
            pltpu.VMEM((count, width), jnp.bfloat16),
            pltpu.VMEM((2 * count, held * units), jnp.bfloat16),
        ],
        cost_estimate=COST,
        compiler_params=params(),
        name="rest_of",
    )(*in_vmem(first, part, w_gate, w_up, w_down))


def sums_kernel(first, second, w_down, mine, *refs):
    *others, hidden = refs
    count = first.shape[0]
    hidden[:count] = first[...]
    hidden[count:] = second[...]
    down_all(hidden, w_down, mine, *others)


def sums_of(first, second, w_down, pieces=1):
    count, width = first.shape[0], w_down.shape[1]
    others = [pltpu.VMEM((count // pieces, width), jnp.bfloat16)] * pieces
    return pl.pallas_call(
        sums_kernel,
        in_specs=[VMEM_SPEC] * 3,
        out_specs=[VMEM_SPEC] * (1 + pieces),
        out_shape=[pltpu.VMEM((count, width), jnp.bfloat16), *others],
        scratch_shapes=[pltpu.VMEM((2 * count, first.shape[1]), jnp.bfloat16)],
        cost_estimate=COST,
        compiler_params=params(),
        name="sums_of",
    )(*in_vmem(first, second, w_down))


def pieces_kernel(mine, *refs):
    *others, out = refs
    piece = others[0].shape[0]
    for i, other in enumerate(others):
        rows = slice(i * piece, (i + 1) * piece)
        out[rows] = (mine[rows].astype(jnp.float32) + other[...].astype(jnp.float32)).astype(out.dtype)


def add_pieces(mine, others):
    return pl.pallas_call(
        pieces_kernel,
        in_specs=[VMEM_SPEC] * (1 + len(others)),
        out_specs=VMEM_SPEC,
        out_shape=pltpu.VMEM(mine.shape, mine.dtype),
        cost_estimate=COST,
        compiler_params=params(8),
        name="add_pieces",
    )(*in_vmem(mine, *others))


def down_units(hidden, w_down, pieces=1):
    count, width = hidden.shape[0] // 2, w_down.shape[1]
    others = [pltpu.VMEM((count // pieces, width), jnp.bfloat16)] * pieces
    return pl.pallas_call(
        down_all,
        in_specs=[VMEM_SPEC] * 2,
        out_specs=[VMEM_SPEC] * (1 + pieces),
        out_shape=[pltpu.VMEM((count, width), jnp.bfloat16), *others],
        cost_estimate=COST,
        compiler_params=params(),
        name="down_units",
    )(*in_vmem(hidden, w_down))


def add_kernel(*refs):
    *parts, out = refs
    width = parts[0].shape[1]
    total = parts[0][...].astype(jnp.float32)
    for part in parts[1:]:
        total += part[:, :width].astype(jnp.float32)
    out[:, :width] = total.astype(out.dtype)
    if out.shape[1] > width:
        out[:, width:] = jnp.zeros((out.shape[0], out.shape[1] - width), out.dtype)


def add(*parts, dtype=jnp.bfloat16, spare=0, cost=COST):
    count, width = parts[0].shape
    return pl.pallas_call(
        add_kernel,
        in_specs=[VMEM_SPEC] * len(parts),
        out_specs=VMEM_SPEC,
        out_shape=pltpu.VMEM((count, width + spare), dtype),
        cost_estimate=cost,
        compiler_params=params(8),
        name="add",
    )(*in_vmem(*parts))


def finish_kernel(*refs, pieces):
    *parts, out, block, sems = refs
    twins, parts = parts[:pieces], parts[pieces:]
    count = block.shape[1]
    copies = []
    for i in range(block.shape[0]):
        start = i * count
        rows = pl.ds(start, count)
        size = twins[0].shape[0]
        total = twins[start // size][pl.ds(start % size, count)].astype(jnp.float32)
        for part in parts:
            total += part[rows].astype(jnp.float32)
        block[i] = total.astype(block.dtype)
        copies.append(pltpu.make_async_copy(block.at[i], out.at[rows], sems.at[i]))
        copies[-1].start()
    for copy in copies:
        copy.wait()


def finish(twins, *parts, blocks=4):
    count, width = parts[0].shape
    return pl.pallas_call(
        functools.partial(finish_kernel, pieces=len(twins)),
        in_specs=[VMEM_SPEC] * (len(twins) + len(parts)),
        out_specs=HBM_SPEC,
        out_shape=jax.ShapeDtypeStruct((count, width), jnp.bfloat16),
        scratch_shapes=[
            pltpu.VMEM((blocks, count // blocks, width), jnp.bfloat16),
            pltpu.SemaphoreType.DMA((blocks,)),
        ],
        cost_estimate=COST,
        compiler_params=params(8),
        name="finish",
    )(*in_vmem(*twins, *parts))


def on_four_chips(tokens, low, high, table, w_gate, w_up, w_down):
    x, y = 2, 4
    barrier = lax.optimization_barrier
    weights = (w_gate, w_up, w_down)
    near_rows, near_table = cross(tokens, x, y), cross(table, x, y)
    gated, rows = gated_units([low, high, flip(low, CORE), flip(high, CORE)], w_gate)
    near_table, near_rows, gated = barrier((near_table, near_rows, gated))
    near = pack(near_rows, near_table)

    far = cross(near, y, x)
    mine_near, other_near = rest_of(units_of([near], *weights), flip(near, CORE), *weights)
    following = cross(join(low, high, table, tokens.shape[1], SPARE), y, x)
    far, mine_near = barrier((far, mine_near))

    far_twin = flip(far, CORE)
    first = units_of([far], w_gate, w_up)
    first, far_twin = barrier((first, far_twin))
    second = units_of([far_twin], w_gate, w_up)
    mine_near, second = barrier((mine_near, second))
    sum_near = add(mine_near, flip(other_near, CORE))
    back = cross(sum_near, x, y)
    following, second = barrier((following, second))
    mine_far, *other_far = sums_of(first, second, w_down, pieces=2)

    following_twin = flip(following, CORE)
    first = units_of([following], w_gate, w_up)
    mine_far, first = barrier((mine_far, first))
    sum_far = add_pieces(mine_far, [flip(other, CORE) for other in other_far])
    sum_far, following_twin, first = barrier((sum_far, following_twin, first))
    relay = cross(sum_far, x, y)
    second = units_of([following_twin], w_gate, w_up)
    second, back = barrier((second, back))
    mine_last, other_last = sums_of(first, second, w_down)
    mine_last, gated = barrier((mine_last, gated))
    hidden = hidden_units(gated, rows, w_up)
    mine_last, hidden = barrier((mine_last, hidden))
    sum_last = add(add(mine_last, relay, dtype=jnp.float32, cost=RELAY), flip(other_last, CORE))
    last = cross(sum_last, y, x)
    mine_own, *other_own = down_units(hidden, w_down, pieces=2)
    return finish([flip(other, CORE) for other in other_own], mine_own, back, last)


def on_any_chips(tokens, low, high, table, *weights):
    own = join(low, high, table, tokens.shape[1])
    offsets = range(2, lax.axis_size("ep"), 2)
    arrived = [flip(own, d) for d in offsets]
    parts = []
    for d, rows in zip([0, *offsets], [own, *arrived]):
        mine, other = rest_of(units_of([rows], *weights[:2]), flip(rows, CORE), *weights)
        other = flip(other, CORE)
        parts += [flip(add(mine, other), d)] if d else [mine, other]
    return finish(parts[:1], *parts[1:])


def body(tokens, experts, gates, w_gate, w_up, w_down):
    n_ep = lax.axis_size("ep")
    n_experts = w_gate.shape[0] * n_ep
    packed = prepare(tokens, experts, gates, n_experts)
    run = on_four_chips if n_ep == 8 else on_any_chips
    return run(tokens, *packed, w_gate, w_up, w_down)


def solution(mesh):
    in_specs = (
        P(("rep", "ep"), None),
        P(("rep", "ep"), None),
        P(("rep", "ep"), None),
        P("ep", None, None),
        P("ep", None, None),
        P("ep", None, None),
    )
    out_specs = P(("rep", "ep"), None)
    return jax.shard_map(body, mesh=mesh, in_specs=in_specs, out_specs=out_specs, check_vma=False)
```

```python
import functools

import jax
import jax.numpy as jnp
from jax import lax
from jax.experimental import pallas as pl
from jax.experimental.pallas import tpu as pltpu
from jax.sharding import PartitionSpec as P

MIB = 2**20
LANES = 128
NT = (((1,), (1,)), ((), ()))
VMEM_SPEC = pl.BlockSpec(memory_space=pltpu.VMEM)
HBM_SPEC = pl.BlockSpec(memory_space=pltpu.HBM)
CORE = 1
PACK = 16
SPARE = LANES
MEDIUM = pl.CostEstimate(flops=0, bytes_accessed=3 * 10**6, transcendentals=0)
RELAY = pl.CostEstimate(flops=2 * 10**9, bytes_accessed=3 * 10**6, transcendentals=0)
LONG = pl.CostEstimate(flops=10**11, bytes_accessed=10**8, transcendentals=0)
COST = pl.CostEstimate(flops=0, bytes_accessed=0, transcendentals=0)


def flip(x, mask):
    n = lax.axis_size("ep")
    return lax.ppermute(x, "ep", [(i, i ^ mask) for i in range(n)])


def cross(x, even, odd):
    n = lax.axis_size("ep")
    return lax.ppermute(x, "ep", [(i, i ^ (odd if i % 2 else even)) for i in range(n)])


def in_vmem(*arrays):
    return [pltpu.with_memory_space_constraint(a, pltpu.VMEM) for a in arrays]


def in_hbm(*arrays):
    return [pltpu.with_memory_space_constraint(a, pltpu.HBM) for a in arrays]


def params(limit=6):
    return pltpu.CompilerParams(vmem_limit_bytes=limit * MIB)


def prepare_kernel(tokens, experts, gates, low, high, table, chosen, weight, sems, *, n_experts):
    count, width = tokens.shape
    groups = count // PACK
    half = groups // 2
    copies = [
        pltpu.make_async_copy(experts, chosen, sems.at[0]),
        pltpu.make_async_copy(gates, weight, sems.at[1]),
    ]
    for j in range(groups):
        rows = tokens.at[pl.ds(j * PACK, PACK)]
        place = (low if j < half else high).at[:, pl.ds(j % half * width, width)]
        copies.append(pltpu.make_async_copy(rows, place, sems.at[2 + j]))
    for copy in copies:
        copy.start()
    copies[0].wait()
    copies[1].wait()
    ids = lax.broadcasted_iota(jnp.int32, (-(-n_experts // LANES) * LANES, count), 0)
    total = jnp.zeros(ids.shape, jnp.float32)
    for k in range(chosen.shape[0]):
        gate = weight[k : k + 1, :].astype(jnp.float32)
        total += jnp.where(ids == chosen[k : k + 1, :], gate, 0.0)
    total = total.T
    blocks = [total[j * PACK : (j + 1) * PACK, :n_experts] for j in range(groups)]
    for out, first, last in ((low, 0, half), (high, half, groups), (table, 0, groups)):
        start = 0 if out is table else half * width
        spare = out.shape[1] - start - (last - first) * n_experts
        values = blocks[first:last] + ([jnp.zeros((PACK, spare), jnp.float32)] if spare else [])
        out[:, start:] = jnp.concatenate(values, axis=1).astype(jnp.bfloat16)
    for copy in copies[2:]:
        copy.wait()


def table_lanes(groups, n_experts):
    return -(-groups * n_experts // LANES) * LANES


def prepare(tokens, experts, gates, n_experts):
    count, width = tokens.shape
    groups = count // PACK
    half = groups // 2 * width + table_lanes(groups // 2, n_experts)
    lanes = [half, half, table_lanes(groups, n_experts)]
    return pl.pallas_call(
        functools.partial(prepare_kernel, n_experts=n_experts),
        in_specs=[HBM_SPEC] * 3,
        out_specs=[VMEM_SPEC] * 3,
        out_shape=[pltpu.VMEM((PACK, size), jnp.bfloat16) for size in lanes],
        scratch_shapes=[
            pltpu.VMEM(experts.shape[::-1], jnp.int32),
            pltpu.VMEM(gates.shape[::-1], jnp.bfloat16),
            pltpu.SemaphoreType.DMA((2 + groups,)),
        ],
        cost_estimate=LONG,
        compiler_params=params(4),
        name="prepare",
    )(*in_hbm(tokens, experts.T, gates.T))


def join_kernel(low, high, table, out, *, width):
    part = low.shape[1] // width * width
    out[:, :part] = low[:, :part]
    out[:, part : 2 * part] = high[:, :part]
    out[:, 2 * part : 2 * part + table.shape[1]] = table[...]
    if out.shape[1] > 2 * part + table.shape[1]:
        spare = out.shape[1] - 2 * part - table.shape[1]
        out[:, 2 * part + table.shape[1] :] = jnp.zeros((PACK, spare), out.dtype)


def join(low, high, table, width, spare=0):
    lanes = low.shape[1] // width * width * 2 + table.shape[1] + spare
    return pl.pallas_call(
        functools.partial(join_kernel, width=width),
        in_specs=[VMEM_SPEC] * 3,
        out_specs=VMEM_SPEC,
        out_shape=pltpu.VMEM((PACK, lanes), low.dtype),
        cost_estimate=COST,
        compiler_params=params(4),
        name="join",
    )(*in_vmem(low, high, table))


def pack_kernel(rows, table, out):
    width = rows.shape[1]
    for j in range(rows.shape[0] // PACK):
        out[:, j * width : (j + 1) * width] = rows[j * PACK : (j + 1) * PACK]
    out[:, rows.shape[0] // PACK * width :] = table[...]


def pack(rows, table):
    return pl.pallas_call(
        pack_kernel,
        in_specs=[VMEM_SPEC] * 2,
        out_specs=VMEM_SPEC,
        out_shape=pltpu.VMEM((PACK, rows.size // PACK + table.shape[1]), rows.dtype),
        cost_estimate=COST,
        compiler_params=params(4),
        name="pack",
    )(*in_vmem(rows, table))


def rows_in(part, width):
    return part.shape[1] // width * PACK


def gather_inputs(parts, rows, held):
    width = rows.shape[1]
    n_experts = held * lax.axis_size("ep")
    base = lax.axis_index("ep") * held
    columns = [[] for _ in range(held)]
    start = 0
    for part in parts:
        groups = part.shape[1] // width
        table = part[:, groups * width :].astype(jnp.float32)
        lane = lax.broadcasted_iota(jnp.int32, table.shape, 1)
        for j in range(groups):
            rows[start : start + PACK] = part[:, j * width : (j + 1) * width]
            start += PACK
            for e in range(held):
                gate = jnp.where(lane == j * n_experts + base + e, table, 0.0)
                columns[e].append(jnp.sum(gate, axis=1, keepdims=True))
    return [jnp.concatenate(column, axis=0) for column in columns]


def gated_of(rows, gate_w, weight):
    gate_act = jnp.dot(rows, gate_w, preferred_element_type=jnp.float32)
    return gate_act * (0.5 * jnp.tanh(0.5 * gate_act) + 0.5) * weight


def hidden_of(rows, gate_w, up_w, weight):
    up_act = jnp.dot(rows, up_w, preferred_element_type=jnp.float32)
    return (gated_of(rows, gate_w, weight) * up_act).astype(jnp.bfloat16)


def down_all(hidden, w_down, mine, *others, tile=512):
    held, width, units = w_down.shape
    count, piece = mine.shape[0], others[0].shape[0]
    for start in range(0, width, tile):
        total = None
        for e in range(held):
            part = lax.dot_general(
                hidden[:, e * units : (e + 1) * units],
                w_down[e, start : start + tile, :],
                NT,
                preferred_element_type=jnp.float32,
            )
            total = part if total is None else total + part
        total = total.astype(jnp.bfloat16)
        mine[:, start : start + tile] = total[:count]
        for i, other in enumerate(others):
            row = count + i * piece
            other[:, start : start + tile] = total[row : row + piece]


def gated_kernel(*refs, parts):
    inputs, (w_gate, gated, rows) = refs[:parts], refs[parts:]
    held, _, units = w_gate.shape
    weights = gather_inputs(inputs, rows, held)
    for e in range(held):
        gated[:, e * units : (e + 1) * units] = gated_of(rows[...], w_gate[e], weights[e])


def gated_units(parts, w_gate):
    held, width, units = w_gate.shape
    count = sum(rows_in(part, width) for part in parts)
    return pl.pallas_call(
        functools.partial(gated_kernel, parts=len(parts)),
        in_specs=[VMEM_SPEC] * (len(parts) + 1),
        out_specs=[VMEM_SPEC] * 2,
        out_shape=[pltpu.VMEM((count, held * units), jnp.float32), pltpu.VMEM((count, width), jnp.bfloat16)],
        cost_estimate=COST,
        compiler_params=params(),
        name="gated_units",
    )(*in_vmem(*parts, w_gate))


def hidden_kernel(gated, rows, w_up, hidden):
    held, _, units = w_up.shape
    for e in range(held):
        block = slice(e * units, (e + 1) * units)
        up_act = jnp.dot(rows[...], w_up[e], preferred_element_type=jnp.float32)
        hidden[:, block] = (gated[:, block] * up_act).astype(jnp.bfloat16)


def hidden_units(gated, rows, w_up):
    return pl.pallas_call(
        hidden_kernel,
        in_specs=[VMEM_SPEC] * 3,
        out_specs=VMEM_SPEC,
        out_shape=pltpu.VMEM(gated.shape, jnp.bfloat16),
        cost_estimate=COST,
        compiler_params=params(),
        name="hidden_units",
    )(*in_vmem(gated, rows, w_up))


def units_kernel(*refs, parts):
    inputs, (w_gate, w_up), (hidden, rows) = refs[:parts], refs[parts : parts + 2], refs[-2:]
    held, _, units = w_gate.shape
    weights = gather_inputs(inputs, rows, held)
    for e in range(held):
        hidden[:, e * units : (e + 1) * units] = hidden_of(rows[...], w_gate[e], w_up[e], weights[e])


def units_of(parts, w_gate, w_up, *others):
    held, width, units = w_gate.shape
    count = sum(rows_in(part, width) for part in parts)
    return pl.pallas_call(
        functools.partial(units_kernel, parts=len(parts)),
        in_specs=[VMEM_SPEC] * (len(parts) + 2 + len(others)),
        out_specs=VMEM_SPEC,
        out_shape=pltpu.VMEM((count, held * units), jnp.bfloat16),
        scratch_shapes=[pltpu.VMEM((count, width), jnp.bfloat16)],
        cost_estimate=COST,
        compiler_params=params(),
        name="units_of",
    )(*in_vmem(*parts, w_gate, w_up, *others))


def rest_kernel(first, part, w_gate, w_up, w_down, mine, other, rows, hidden):
    held, _, units = w_gate.shape
    count = first.shape[0]
    weights = gather_inputs([part], rows, held)
    for e in range(held):
        block = slice(e * units, (e + 1) * units)
        hidden[:count, block] = first[:, block]
        hidden[count:, block] = hidden_of(rows[...], w_gate[e], w_up[e], weights[e])
    down_all(hidden, w_down, mine, other)


def rest_of(first, part, w_gate, w_up, w_down):
    held, width, units = w_gate.shape
    count = rows_in(part, width)
    return pl.pallas_call(
        rest_kernel,
        in_specs=[VMEM_SPEC] * 5,
        out_specs=[VMEM_SPEC] * 2,
        out_shape=[pltpu.VMEM((count, width), jnp.bfloat16)] * 2,
        scratch_shapes=[
            pltpu.VMEM((count, width), jnp.bfloat16),
            pltpu.VMEM((2 * count, held * units), jnp.bfloat16),
        ],
        cost_estimate=COST,
        compiler_params=params(),
        name="rest_of",
    )(*in_vmem(first, part, w_gate, w_up, w_down))


def sums_kernel(first, second, w_down, mine, *refs):
    *others, hidden = refs
    count = first.shape[0]
    hidden[:count] = first[...]
    hidden[count:] = second[...]
    down_all(hidden, w_down, mine, *others)


def sums_of(first, second, w_down, pieces=1):
    count, width = first.shape[0], w_down.shape[1]
    others = [pltpu.VMEM((count // pieces, width), jnp.bfloat16)] * pieces
    return pl.pallas_call(
        sums_kernel,
        in_specs=[VMEM_SPEC] * 3,
        out_specs=[VMEM_SPEC] * (1 + pieces),
        out_shape=[pltpu.VMEM((count, width), jnp.bfloat16), *others],
        scratch_shapes=[pltpu.VMEM((2 * count, first.shape[1]), jnp.bfloat16)],
        cost_estimate=COST,
        compiler_params=params(),
        name="sums_of",
    )(*in_vmem(first, second, w_down))


def pieces_kernel(mine, *refs):
    *others, out = refs
    piece = others[0].shape[0]
    for i, other in enumerate(others):
        rows = slice(i * piece, (i + 1) * piece)
        out[rows] = (mine[rows].astype(jnp.float32) + other[...].astype(jnp.float32)).astype(out.dtype)


def add_pieces(mine, others):
    return pl.pallas_call(
        pieces_kernel,
        in_specs=[VMEM_SPEC] * (1 + len(others)),
        out_specs=VMEM_SPEC,
        out_shape=pltpu.VMEM(mine.shape, mine.dtype),
        cost_estimate=COST,
        compiler_params=params(8),
        name="add_pieces",
    )(*in_vmem(mine, *others))


def down_units(hidden, w_down, pieces=1):
    count, width = hidden.shape[0] // 2, w_down.shape[1]
    others = [pltpu.VMEM((count // pieces, width), jnp.bfloat16)] * pieces
    return pl.pallas_call(
        down_all,
        in_specs=[VMEM_SPEC] * 2,
        out_specs=[VMEM_SPEC] * (1 + pieces),
        out_shape=[pltpu.VMEM((count, width), jnp.bfloat16), *others],
        cost_estimate=COST,
        compiler_params=params(),
        name="down_units",
    )(*in_vmem(hidden, w_down))


def add_kernel(*refs):
    *parts, out = refs
    width = parts[0].shape[1]
    total = parts[0][...].astype(jnp.float32)
    for part in parts[1:]:
        total += part[:, :width].astype(jnp.float32)
    out[:, :width] = total.astype(out.dtype)
    if out.shape[1] > width:
        out[:, width:] = jnp.zeros((out.shape[0], out.shape[1] - width), out.dtype)


def add(*parts, dtype=jnp.bfloat16, spare=0, cost=COST):
    count, width = parts[0].shape
    return pl.pallas_call(
        add_kernel,
        in_specs=[VMEM_SPEC] * len(parts),
        out_specs=VMEM_SPEC,
        out_shape=pltpu.VMEM((count, width + spare), dtype),
        cost_estimate=cost,
        compiler_params=params(8),
        name="add",
    )(*in_vmem(*parts))


def finish_kernel(*refs, pieces):
    *parts, out, block, sems = refs
    twins, parts = parts[:pieces], parts[pieces:]
    count = block.shape[1]
    copies = []
    for i in range(block.shape[0]):
        start = i * count
        rows = pl.ds(start, count)
        size = twins[0].shape[0]
        total = twins[start // size][pl.ds(start % size, count)].astype(jnp.float32)
        for part in parts:
            total += part[rows].astype(jnp.float32)
        block[i] = total.astype(block.dtype)
        copies.append(pltpu.make_async_copy(block.at[i], out.at[rows], sems.at[i]))
        copies[-1].start()
    for copy in copies:
        copy.wait()


def finish(twins, *parts, blocks=4):
    count, width = parts[0].shape
    return pl.pallas_call(
        functools.partial(finish_kernel, pieces=len(twins)),
        in_specs=[VMEM_SPEC] * (len(twins) + len(parts)),
        out_specs=HBM_SPEC,
        out_shape=jax.ShapeDtypeStruct((count, width), jnp.bfloat16),
        scratch_shapes=[
            pltpu.VMEM((blocks, count // blocks, width), jnp.bfloat16),
            pltpu.SemaphoreType.DMA((blocks,)),
        ],
        cost_estimate=COST,
        compiler_params=params(8),
        name="finish",
    )(*in_vmem(*twins, *parts))


def on_four_chips(tokens, low, high, table, w_gate, w_up, w_down):
    x, y = 2, 4
    barrier = lax.optimization_barrier
    weights = (w_gate, w_up, w_down)
    near_rows, near_table = cross(tokens, x, y), cross(table, x, y)
    gated, rows = gated_units([low, high, flip(low, CORE), flip(high, CORE)], w_gate)
    near_table, near_rows, gated = barrier((near_table, near_rows, gated))
    near = pack(near_rows, near_table)

    far = cross(near, y, x)
    mine_near, other_near = rest_of(units_of([near], *weights), flip(near, CORE), *weights)
    following = cross(join(low, high, table, tokens.shape[1], SPARE), y, x)
    far, mine_near = barrier((far, mine_near))

    far_twin = flip(far, CORE)
    first = units_of([far], w_gate, w_up)
    first, far_twin = barrier((first, far_twin))
    second = units_of([far_twin], w_gate, w_up)
    mine_near, second = barrier((mine_near, second))
    sum_near = add(mine_near, flip(other_near, CORE))
    back = cross(sum_near, x, y)
    following, second = barrier((following, second))
    mine_far, *other_far = sums_of(first, second, w_down, pieces=2)

    following_twin = flip(following, CORE)
    first = units_of([following], w_gate, w_up)
    mine_far, first = barrier((mine_far, first))
    sum_far = add_pieces(mine_far, [flip(other, CORE) for other in other_far])
    sum_far, following_twin, first = barrier((sum_far, following_twin, first))
    relay = cross(sum_far, x, y)
    second = units_of([following_twin], w_gate, w_up)
    second, back = barrier((second, back))
    mine_last, other_last = sums_of(first, second, w_down)
    mine_last, gated = barrier((mine_last, gated))
    hidden = hidden_units(gated, rows, w_up)
    mine_last, hidden = barrier((mine_last, hidden))
    sum_last = add(add(mine_last, relay, dtype=jnp.float32, cost=RELAY), flip(other_last, CORE))
    last = cross(sum_last, y, x)
    mine_own, *other_own = down_units(hidden, w_down, pieces=2)
    return finish([flip(other, CORE) for other in other_own], mine_own, back, last)


def on_any_chips(tokens, low, high, table, *weights):
    own = join(low, high, table, tokens.shape[1])
    offsets = range(2, lax.axis_size("ep"), 2)
    arrived = [flip(own, d) for d in offsets]
    parts = []
    for d, rows in zip([0, *offsets], [own, *arrived]):
        mine, other = rest_of(units_of([rows], *weights[:2]), flip(rows, CORE), *weights)
        other = flip(other, CORE)
        parts += [flip(add(mine, other), d)] if d else [mine, other]
    return finish(parts[:1], *parts[1:])


def body(tokens, experts, gates, w_gate, w_up, w_down):
    n_ep = lax.axis_size("ep")
    n_experts = w_gate.shape[0] * n_ep
    packed = prepare(tokens, experts, gates, n_experts)
    run = on_four_chips if n_ep == 8 else on_any_chips
    return run(tokens, *packed, w_gate, w_up, w_down)


def solution(mesh):
    in_specs = (
        P(("rep", "ep"), None),
        P(("rep", "ep"), None),
        P(("rep", "ep"), None),
        P("ep", None, None),
        P("ep", None, None),
        P("ep", None, None),
    )
    out_specs = P(("rep", "ep"), None)
    return jax.shard_map(body, mesh=mesh, in_specs=in_specs, out_specs=out_specs, check_vma=False)
```

```python
import functools

import jax
import jax.numpy as jnp
from jax import lax
from jax.experimental import pallas as pl
from jax.experimental.pallas import tpu as pltpu
from jax.sharding import PartitionSpec as P

MIB = 2**20
LANES = 128
NT = (((1,), (1,)), ((), ()))
VMEM_SPEC = pl.BlockSpec(memory_space=pltpu.VMEM)
HBM_SPEC = pl.BlockSpec(memory_space=pltpu.HBM)
CORE = 1
PACK = 16
SPARE = LANES
MEDIUM = pl.CostEstimate(flops=0, bytes_accessed=3 * 10**6, transcendentals=0)
RELAY = pl.CostEstimate(flops=2 * 10**9, bytes_accessed=3 * 10**6, transcendentals=0)
LONG = pl.CostEstimate(flops=10**11, bytes_accessed=10**8, transcendentals=0)
COST = pl.CostEstimate(flops=0, bytes_accessed=0, transcendentals=0)


def flip(x, mask):
    n = lax.axis_size("ep")
    return lax.ppermute(x, "ep", [(i, i ^ mask) for i in range(n)])


def cross(x, even, odd):
    n = lax.axis_size("ep")
    return lax.ppermute(x, "ep", [(i, i ^ (odd if i % 2 else even)) for i in range(n)])


def in_vmem(*arrays):
    return [pltpu.with_memory_space_constraint(a, pltpu.VMEM) for a in arrays]


def in_hbm(*arrays):
    return [pltpu.with_memory_space_constraint(a, pltpu.HBM) for a in arrays]


def params(limit=6):
    return pltpu.CompilerParams(vmem_limit_bytes=limit * MIB)


def prepare_kernel(tokens, experts, gates, low, high, table, chosen, weight, sems, *, n_experts):
    count, width = tokens.shape
    groups = count // PACK
    half = groups // 2
    copies = [
        pltpu.make_async_copy(experts, chosen, sems.at[0]),
        pltpu.make_async_copy(gates, weight, sems.at[1]),
    ]
    for j in range(groups):
        rows = tokens.at[pl.ds(j * PACK, PACK)]
        place = (low if j < half else high).at[:, pl.ds(j % half * width, width)]
        copies.append(pltpu.make_async_copy(rows, place, sems.at[2 + j]))
    for copy in copies:
        copy.start()
    copies[0].wait()
    copies[1].wait()
    ids = lax.broadcasted_iota(jnp.int32, (-(-n_experts // LANES) * LANES, count), 0)
    total = jnp.zeros(ids.shape, jnp.float32)
    for k in range(chosen.shape[0]):
        gate = weight[k : k + 1, :].astype(jnp.float32)
        total += jnp.where(ids == chosen[k : k + 1, :], gate, 0.0)
    total = total.T
    blocks = [total[j * PACK : (j + 1) * PACK, :n_experts] for j in range(groups)]
    for out, first, last in ((low, 0, half), (high, half, groups), (table, 0, groups)):
        start = 0 if out is table else half * width
        spare = out.shape[1] - start - (last - first) * n_experts
        values = blocks[first:last] + ([jnp.zeros((PACK, spare), jnp.float32)] if spare else [])
        out[:, start:] = jnp.concatenate(values, axis=1).astype(jnp.bfloat16)
    for copy in copies[2:]:
        copy.wait()


def table_lanes(groups, n_experts):
    return -(-groups * n_experts // LANES) * LANES


def prepare(tokens, experts, gates, n_experts):
    count, width = tokens.shape
    groups = count // PACK
    half = groups // 2 * width + table_lanes(groups // 2, n_experts)
    lanes = [half, half, table_lanes(groups, n_experts)]
    return pl.pallas_call(
        functools.partial(prepare_kernel, n_experts=n_experts),
        in_specs=[HBM_SPEC] * 3,
        out_specs=[VMEM_SPEC] * 3,
        out_shape=[pltpu.VMEM((PACK, size), jnp.bfloat16) for size in lanes],
        scratch_shapes=[
            pltpu.VMEM(experts.shape[::-1], jnp.int32),
            pltpu.VMEM(gates.shape[::-1], jnp.bfloat16),
            pltpu.SemaphoreType.DMA((2 + groups,)),
        ],
        cost_estimate=LONG,
        compiler_params=params(4),
        name="prepare",
    )(*in_hbm(tokens, experts.T, gates.T))


def join_kernel(low, high, table, out, *, width):
    part = low.shape[1] // width * width
    out[:, :part] = low[:, :part]
    out[:, part : 2 * part] = high[:, :part]
    out[:, 2 * part : 2 * part + table.shape[1]] = table[...]
    if out.shape[1] > 2 * part + table.shape[1]:
        spare = out.shape[1] - 2 * part - table.shape[1]
        out[:, 2 * part + table.shape[1] :] = jnp.zeros((PACK, spare), out.dtype)


def join(low, high, table, width, spare=0):
    lanes = low.shape[1] // width * width * 2 + table.shape[1] + spare
    return pl.pallas_call(
        functools.partial(join_kernel, width=width),
        in_specs=[VMEM_SPEC] * 3,
        out_specs=VMEM_SPEC,
        out_shape=pltpu.VMEM((PACK, lanes), low.dtype),
        cost_estimate=COST,
        compiler_params=params(4),
        name="join",
    )(*in_vmem(low, high, table))


def pack_kernel(rows, table, out):
    width = rows.shape[1]
    for j in range(rows.shape[0] // PACK):
        out[:, j * width : (j + 1) * width] = rows[j * PACK : (j + 1) * PACK]
    out[:, rows.shape[0] // PACK * width :] = table[...]


def pack(rows, table):
    return pl.pallas_call(
        pack_kernel,
        in_specs=[VMEM_SPEC] * 2,
        out_specs=VMEM_SPEC,
        out_shape=pltpu.VMEM((PACK, rows.size // PACK + table.shape[1]), rows.dtype),
        cost_estimate=COST,
        compiler_params=params(4),
        name="pack",
    )(*in_vmem(rows, table))


def rows_in(part, width):
    return part.shape[1] // width * PACK


def gather_inputs(parts, rows, held):
    width = rows.shape[1]
    n_experts = held * lax.axis_size("ep")
    base = lax.axis_index("ep") * held
    columns = [[] for _ in range(held)]
    start = 0
    for part in parts:
        groups = part.shape[1] // width
        table = part[:, groups * width :].astype(jnp.float32)
        lane = lax.broadcasted_iota(jnp.int32, table.shape, 1)
        for j in range(groups):
            rows[start : start + PACK] = part[:, j * width : (j + 1) * width]
            start += PACK
            for e in range(held):
                gate = jnp.where(lane == j * n_experts + base + e, table, 0.0)
                columns[e].append(jnp.sum(gate, axis=1, keepdims=True))
    return [jnp.concatenate(column, axis=0) for column in columns]


def gated_of(rows, gate_w, weight):
    gate_act = jnp.dot(rows, gate_w, preferred_element_type=jnp.float32)
    return gate_act * (0.5 * jnp.tanh(0.5 * gate_act) + 0.5) * weight


def hidden_of(rows, gate_w, up_w, weight):
    up_act = jnp.dot(rows, up_w, preferred_element_type=jnp.float32)
    return (gated_of(rows, gate_w, weight) * up_act).astype(jnp.bfloat16)


def down_all(hidden, w_down, mine, *others, tile=512):
    held, width, units = w_down.shape
    count, piece = mine.shape[0], others[0].shape[0]
    for start in range(0, width, tile):
        total = None
        for e in range(held):
            part = lax.dot_general(
                hidden[:, e * units : (e + 1) * units],
                w_down[e, start : start + tile, :],
                NT,
                preferred_element_type=jnp.float32,
            )
            total = part if total is None else total + part
        total = total.astype(jnp.bfloat16)
        mine[:, start : start + tile] = total[:count]
        for i, other in enumerate(others):
            row = count + i * piece
            other[:, start : start + tile] = total[row : row + piece]


def gated_kernel(*refs, parts):
    inputs, (w_gate, gated, rows) = refs[:parts], refs[parts:]
    held, _, units = w_gate.shape
    weights = gather_inputs(inputs, rows, held)
    for e in range(held):
        gated[:, e * units : (e + 1) * units] = gated_of(rows[...], w_gate[e], weights[e])


def gated_units(parts, w_gate):
    held, width, units = w_gate.shape
    count = sum(rows_in(part, width) for part in parts)
    return pl.pallas_call(
        functools.partial(gated_kernel, parts=len(parts)),
        in_specs=[VMEM_SPEC] * (len(parts) + 1),
        out_specs=[VMEM_SPEC] * 2,
        out_shape=[pltpu.VMEM((count, held * units), jnp.float32), pltpu.VMEM((count, width), jnp.bfloat16)],
        cost_estimate=COST,
        compiler_params=params(),
        name="gated_units",
    )(*in_vmem(*parts, w_gate))


def hidden_kernel(gated, rows, w_up, hidden):
    held, _, units = w_up.shape
    for e in range(held):
        block = slice(e * units, (e + 1) * units)
        up_act = jnp.dot(rows[...], w_up[e], preferred_element_type=jnp.float32)
        hidden[:, block] = (gated[:, block] * up_act).astype(jnp.bfloat16)


def hidden_units(gated, rows, w_up):
    return pl.pallas_call(
        hidden_kernel,
        in_specs=[VMEM_SPEC] * 3,
        out_specs=VMEM_SPEC,
        out_shape=pltpu.VMEM(gated.shape, jnp.bfloat16),
        cost_estimate=COST,
        compiler_params=params(),
        name="hidden_units",
    )(*in_vmem(gated, rows, w_up))


def units_kernel(*refs, parts):
    inputs, (w_gate, w_up), (hidden, rows) = refs[:parts], refs[parts : parts + 2], refs[-2:]
    held, _, units = w_gate.shape
    weights = gather_inputs(inputs, rows, held)
    for e in range(held):
        hidden[:, e * units : (e + 1) * units] = hidden_of(rows[...], w_gate[e], w_up[e], weights[e])


def units_of(parts, w_gate, w_up, *others):
    held, width, units = w_gate.shape
    count = sum(rows_in(part, width) for part in parts)
    return pl.pallas_call(
        functools.partial(units_kernel, parts=len(parts)),
        in_specs=[VMEM_SPEC] * (len(parts) + 2 + len(others)),
        out_specs=VMEM_SPEC,
        out_shape=pltpu.VMEM((count, held * units), jnp.bfloat16),
        scratch_shapes=[pltpu.VMEM((count, width), jnp.bfloat16)],
        cost_estimate=COST,
        compiler_params=params(),
        name="units_of",
    )(*in_vmem(*parts, w_gate, w_up, *others))


def both_kernel(gated, gated_rows, part, w_gate, w_up, first, second, rows):
    held, _, units = w_gate.shape
    weights = gather_inputs([part], rows, held)
    for e in range(held):
        block = slice(e * units, (e + 1) * units)
        up_act = jnp.dot(gated_rows[...], w_up[e], preferred_element_type=jnp.float32)
        first[:, block] = (gated[:, block] * up_act).astype(jnp.bfloat16)
        second[:, block] = hidden_of(rows[...], w_gate[e], w_up[e], weights[e])


def both_units(gated, gated_rows, part, w_gate, w_up):
    half = pltpu.VMEM(gated.shape, jnp.bfloat16)
    return pl.pallas_call(
        both_kernel,
        in_specs=[VMEM_SPEC] * 5,
        out_specs=[VMEM_SPEC] * 2,
        out_shape=[half, half],
        scratch_shapes=[pltpu.VMEM(gated_rows.shape, jnp.bfloat16)],
        cost_estimate=COST,
        compiler_params=params(),
        name="both_units",
    )(*in_vmem(gated, gated_rows, part, w_gate, w_up))


def rest_kernel(first, part, w_gate, w_up, w_down, mine, other, rows, hidden):
    held, _, units = w_gate.shape
    count = first.shape[0]
    weights = gather_inputs([part], rows, held)
    for e in range(held):
        block = slice(e * units, (e + 1) * units)
        hidden[:count, block] = first[:, block]
        hidden[count:, block] = hidden_of(rows[...], w_gate[e], w_up[e], weights[e])
    down_all(hidden, w_down, mine, other)


def rest_of(first, part, w_gate, w_up, w_down):
    held, width, units = w_gate.shape
    count = rows_in(part, width)
    return pl.pallas_call(
        rest_kernel,
        in_specs=[VMEM_SPEC] * 5,
        out_specs=[VMEM_SPEC] * 2,
        out_shape=[pltpu.VMEM((count, width), jnp.bfloat16)] * 2,
        scratch_shapes=[
            pltpu.VMEM((count, width), jnp.bfloat16),
            pltpu.VMEM((2 * count, held * units), jnp.bfloat16),
        ],
        cost_estimate=COST,
        compiler_params=params(),
        name="rest_of",
    )(*in_vmem(first, part, w_gate, w_up, w_down))


def sums_kernel(first, second, w_down, mine, *refs):
    *others, hidden = refs
    count = first.shape[0]
    hidden[:count] = first[...]
    hidden[count:] = second[...]
    down_all(hidden, w_down, mine, *others)


def sums_of(first, second, w_down, pieces=1):
    count, width = first.shape[0], w_down.shape[1]
    others = [pltpu.VMEM((count // pieces, width), jnp.bfloat16)] * pieces
    return pl.pallas_call(
        sums_kernel,
        in_specs=[VMEM_SPEC] * 3,
        out_specs=[VMEM_SPEC] * (1 + pieces),
        out_shape=[pltpu.VMEM((count, width), jnp.bfloat16), *others],
        scratch_shapes=[pltpu.VMEM((2 * count, first.shape[1]), jnp.bfloat16)],
        cost_estimate=COST,
        compiler_params=params(),
        name="sums_of",
    )(*in_vmem(first, second, w_down))


def pieces_kernel(mine, *refs):
    *others, out = refs
    piece = others[0].shape[0]
    for i, other in enumerate(others):
        rows = slice(i * piece, (i + 1) * piece)
        out[rows] = (mine[rows].astype(jnp.float32) + other[...].astype(jnp.float32)).astype(out.dtype)


def add_pieces(mine, others):
    return pl.pallas_call(
        pieces_kernel,
        in_specs=[VMEM_SPEC] * (1 + len(others)),
        out_specs=VMEM_SPEC,
        out_shape=pltpu.VMEM(mine.shape, mine.dtype),
        cost_estimate=COST,
        compiler_params=params(8),
        name="add_pieces",
    )(*in_vmem(mine, *others))


def down_units(hidden, w_down, pieces=1):
    count, width = hidden.shape[0] // 2, w_down.shape[1]
    others = [pltpu.VMEM((count // pieces, width), jnp.bfloat16)] * pieces
    return pl.pallas_call(
        down_all,
        in_specs=[VMEM_SPEC] * 2,
        out_specs=[VMEM_SPEC] * (1 + pieces),
        out_shape=[pltpu.VMEM((count, width), jnp.bfloat16), *others],
        cost_estimate=COST,
        compiler_params=params(),
        name="down_units",
    )(*in_vmem(hidden, w_down))


def add_kernel(*refs):
    *parts, out = refs
    width = parts[0].shape[1]
    total = parts[0][...].astype(jnp.float32)
    for part in parts[1:]:
        total += part[:, :width].astype(jnp.float32)
    out[:, :width] = total.astype(out.dtype)
    if out.shape[1] > width:
        out[:, width:] = jnp.zeros((out.shape[0], out.shape[1] - width), out.dtype)


def add(*parts, dtype=jnp.bfloat16, spare=0, cost=COST):
    count, width = parts[0].shape
    return pl.pallas_call(
        add_kernel,
        in_specs=[VMEM_SPEC] * len(parts),
        out_specs=VMEM_SPEC,
        out_shape=pltpu.VMEM((count, width + spare), dtype),
        cost_estimate=cost,
        compiler_params=params(8),
        name="add",
    )(*in_vmem(*parts))


def finish_kernel(*refs, pieces):
    *parts, out, block, sems = refs
    twins, parts = parts[:pieces], parts[pieces:]
    count = block.shape[1]
    copies = []
    for i in range(block.shape[0]):
        start = i * count
        rows = pl.ds(start, count)
        size = twins[0].shape[0]
        total = twins[start // size][pl.ds(start % size, count)].astype(jnp.float32)
        for part in parts:
            total += part[rows].astype(jnp.float32)
        block[i] = total.astype(block.dtype)
        copies.append(pltpu.make_async_copy(block.at[i], out.at[rows], sems.at[i]))
        copies[-1].start()
    for copy in copies:
        copy.wait()


def finish(twins, *parts, blocks=4):
    count, width = parts[0].shape
    return pl.pallas_call(
        functools.partial(finish_kernel, pieces=len(twins)),
        in_specs=[VMEM_SPEC] * (len(twins) + len(parts)),
        out_specs=HBM_SPEC,
        out_shape=jax.ShapeDtypeStruct((count, width), jnp.bfloat16),
        scratch_shapes=[
            pltpu.VMEM((blocks, count // blocks, width), jnp.bfloat16),
            pltpu.SemaphoreType.DMA((blocks,)),
        ],
        cost_estimate=COST,
        compiler_params=params(8),
        name="finish",
    )(*in_vmem(*twins, *parts))


def on_four_chips(tokens, low, high, table, w_gate, w_up, w_down):
    x, y = 2, 4
    barrier = lax.optimization_barrier
    weights = (w_gate, w_up, w_down)
    near_rows, near_table = cross(tokens, x, y), cross(table, x, y)
    gated, rows = gated_units([low, high, flip(low, CORE), flip(high, CORE)], w_gate)
    near_table, near_rows, gated = barrier((near_table, near_rows, gated))
    near = pack(near_rows, near_table)

    far = cross(near, y, x)
    mine_near, other_near = rest_of(units_of([near], *weights), flip(near, CORE), *weights)
    following = cross(join(low, high, table, tokens.shape[1], SPARE), y, x)
    far, mine_near = barrier((far, mine_near))

    far_twin = flip(far, CORE)
    first = units_of([far], w_gate, w_up)
    first, far_twin = barrier((first, far_twin))
    second = units_of([far_twin], w_gate, w_up)
    mine_near, second = barrier((mine_near, second))
    sum_near = add(mine_near, flip(other_near, CORE))
    back = cross(sum_near, x, y)
    following, second = barrier((following, second))
    mine_far, *other_far = sums_of(first, second, w_down, pieces=2)

    following_twin = flip(following, CORE)
    first, first_rows = gated_units([following], w_gate)
    mine_far, first = barrier((mine_far, first))
    sum_far = add_pieces(mine_far, [flip(other, CORE) for other in other_far])
    sum_far, following_twin, first = barrier((sum_far, following_twin, first))
    relay = cross(sum_far, x, y)
    first, second = both_units(first, first_rows, following_twin, w_gate, w_up)
    second, back = barrier((second, back))
    mine_last, other_last = sums_of(first, second, w_down)
    sum_last = add(add(mine_last, relay, dtype=jnp.float32, cost=RELAY), flip(other_last, CORE))
    last = cross(sum_last, y, x)
    hidden = hidden_units(gated, rows, w_up)
    mine_own, *other_own = down_units(hidden, w_down, pieces=2)
    return finish([flip(other, CORE) for other in other_own], mine_own, back, last)


def on_any_chips(tokens, low, high, table, *weights):
    own = join(low, high, table, tokens.shape[1])
    offsets = range(2, lax.axis_size("ep"), 2)
    arrived = [flip(own, d) for d in offsets]
    parts = []
    for d, rows in zip([0, *offsets], [own, *arrived]):
        mine, other = rest_of(units_of([rows], *weights[:2]), flip(rows, CORE), *weights)
        other = flip(other, CORE)
        parts += [flip(add(mine, other), d)] if d else [mine, other]
    return finish(parts[:1], *parts[1:])


def body(tokens, experts, gates, w_gate, w_up, w_down):
    n_ep = lax.axis_size("ep")
    n_experts = w_gate.shape[0] * n_ep
    packed = prepare(tokens, experts, gates, n_experts)
    run = on_four_chips if n_ep == 8 else on_any_chips
    return run(tokens, *packed, w_gate, w_up, w_down)


def solution(mesh):
    in_specs = (
        P(("rep", "ep"), None),
        P(("rep", "ep"), None),
        P(("rep", "ep"), None),
        P("ep", None, None),
        P("ep", None, None),
        P("ep", None, None),
    )
    out_specs = P(("rep", "ep"), None)
    return jax.shard_map(body, mesh=mesh, in_specs=in_specs, out_specs=out_specs, check_vma=False)
```

```python
import functools

import jax
import jax.numpy as jnp
from jax import lax
from jax.experimental import pallas as pl
from jax.experimental.pallas import tpu as pltpu
from jax.sharding import PartitionSpec as P

MIB = 2**20
LANES = 128
NT = (((1,), (1,)), ((), ()))
VMEM_SPEC = pl.BlockSpec(memory_space=pltpu.VMEM)
HBM_SPEC = pl.BlockSpec(memory_space=pltpu.HBM)
CORE = 1
PACK = 16
SPARE = LANES
MEDIUM = pl.CostEstimate(flops=0, bytes_accessed=3 * 10**6, transcendentals=0)
RELAY = pl.CostEstimate(flops=2 * 10**9, bytes_accessed=3 * 10**6, transcendentals=0)
LONG = pl.CostEstimate(flops=10**11, bytes_accessed=10**8, transcendentals=0)
COST = pl.CostEstimate(flops=0, bytes_accessed=0, transcendentals=0)


def flip(x, mask):
    n = lax.axis_size("ep")
    return lax.ppermute(x, "ep", [(i, i ^ mask) for i in range(n)])


def cross(x, even, odd):
    n = lax.axis_size("ep")
    return lax.ppermute(x, "ep", [(i, i ^ (odd if i % 2 else even)) for i in range(n)])


def in_vmem(*arrays):
    return [pltpu.with_memory_space_constraint(a, pltpu.VMEM) for a in arrays]


def in_hbm(*arrays):
    return [pltpu.with_memory_space_constraint(a, pltpu.HBM) for a in arrays]


def params(limit=6):
    return pltpu.CompilerParams(vmem_limit_bytes=limit * MIB)


def prepare_kernel(tokens, experts, gates, low, high, table, chosen, weight, sems, *, n_experts):
    count, width = tokens.shape
    groups = count // PACK
    half = groups // 2
    copies = [
        pltpu.make_async_copy(experts, chosen, sems.at[0]),
        pltpu.make_async_copy(gates, weight, sems.at[1]),
    ]
    for j in range(groups):
        rows = tokens.at[pl.ds(j * PACK, PACK)]
        place = (low if j < half else high).at[:, pl.ds(j % half * width, width)]
        copies.append(pltpu.make_async_copy(rows, place, sems.at[2 + j]))
    for copy in copies:
        copy.start()
    copies[0].wait()
    copies[1].wait()
    ids = lax.broadcasted_iota(jnp.int32, (-(-n_experts // LANES) * LANES, count), 0)
    total = jnp.zeros(ids.shape, jnp.float32)
    for k in range(chosen.shape[0]):
        gate = weight[k : k + 1, :].astype(jnp.float32)
        total += jnp.where(ids == chosen[k : k + 1, :], gate, 0.0)
    total = total.T
    blocks = [total[j * PACK : (j + 1) * PACK, :n_experts] for j in range(groups)]
    for out, first, last in ((low, 0, half), (high, half, groups), (table, 0, groups)):
        start = 0 if out is table else half * width
        spare = out.shape[1] - start - (last - first) * n_experts
        values = blocks[first:last] + ([jnp.zeros((PACK, spare), jnp.float32)] if spare else [])
        out[:, start:] = jnp.concatenate(values, axis=1).astype(jnp.bfloat16)
    for copy in copies[2:]:
        copy.wait()


def table_lanes(groups, n_experts):
    return -(-groups * n_experts // LANES) * LANES


def prepare(tokens, experts, gates, n_experts):
    count, width = tokens.shape
    groups = count // PACK
    half = groups // 2 * width + table_lanes(groups // 2, n_experts)
    lanes = [half, half, table_lanes(groups, n_experts)]
    return pl.pallas_call(
        functools.partial(prepare_kernel, n_experts=n_experts),
        in_specs=[HBM_SPEC] * 3,
        out_specs=[VMEM_SPEC] * 3,
        out_shape=[pltpu.VMEM((PACK, size), jnp.bfloat16) for size in lanes],
        scratch_shapes=[
            pltpu.VMEM(experts.shape[::-1], jnp.int32),
            pltpu.VMEM(gates.shape[::-1], jnp.bfloat16),
            pltpu.SemaphoreType.DMA((2 + groups,)),
        ],
        cost_estimate=LONG,
        compiler_params=params(4),
        name="prepare",
    )(*in_hbm(tokens, experts.T, gates.T))


def join_kernel(low, high, table, out, *, width):
    part = low.shape[1] // width * width
    out[:, :part] = low[:, :part]
    out[:, part : 2 * part] = high[:, :part]
    out[:, 2 * part : 2 * part + table.shape[1]] = table[...]
    if out.shape[1] > 2 * part + table.shape[1]:
        spare = out.shape[1] - 2 * part - table.shape[1]
        out[:, 2 * part + table.shape[1] :] = jnp.zeros((PACK, spare), out.dtype)


def join(low, high, table, width, spare=0):
    lanes = low.shape[1] // width * width * 2 + table.shape[1] + spare
    return pl.pallas_call(
        functools.partial(join_kernel, width=width),
        in_specs=[VMEM_SPEC] * 3,
        out_specs=VMEM_SPEC,
        out_shape=pltpu.VMEM((PACK, lanes), low.dtype),
        cost_estimate=COST,
        compiler_params=params(4),
        name="join",
    )(*in_vmem(low, high, table))


def pack_kernel(rows, table, out):
    width = rows.shape[1]
    for j in range(rows.shape[0] // PACK):
        out[:, j * width : (j + 1) * width] = rows[j * PACK : (j + 1) * PACK]
    out[:, rows.shape[0] // PACK * width :] = table[...]


def pack(rows, table):
    return pl.pallas_call(
        pack_kernel,
        in_specs=[VMEM_SPEC] * 2,
        out_specs=VMEM_SPEC,
        out_shape=pltpu.VMEM((PACK, rows.size // PACK + table.shape[1]), rows.dtype),
        cost_estimate=COST,
        compiler_params=params(4),
        name="pack",
    )(*in_vmem(rows, table))


def rows_in(part, width):
    return part.shape[1] // width * PACK


def gather_inputs(parts, rows, held):
    width = rows.shape[1]
    n_experts = held * lax.axis_size("ep")
    base = lax.axis_index("ep") * held
    columns = [[] for _ in range(held)]
    start = 0
    for part in parts:
        groups = part.shape[1] // width
        table = part[:, groups * width :].astype(jnp.float32)
        lane = lax.broadcasted_iota(jnp.int32, table.shape, 1)
        for j in range(groups):
            rows[start : start + PACK] = part[:, j * width : (j + 1) * width]
            start += PACK
            for e in range(held):
                gate = jnp.where(lane == j * n_experts + base + e, table, 0.0)
                columns[e].append(jnp.sum(gate, axis=1, keepdims=True))
    return [jnp.concatenate(column, axis=0) for column in columns]


def gated_of(rows, gate_w, weight):
    gate_act = jnp.dot(rows, gate_w, preferred_element_type=jnp.float32)
    return gate_act * (0.5 * jnp.tanh(0.5 * gate_act) + 0.5) * weight


def hidden_of(rows, gate_w, up_w, weight):
    up_act = jnp.dot(rows, up_w, preferred_element_type=jnp.float32)
    return (gated_of(rows, gate_w, weight) * up_act).astype(jnp.bfloat16)


def down_all(hidden, w_down, mine, *others, tile=512):
    held, width, units = w_down.shape
    count, piece = mine.shape[0], others[0].shape[0]
    for start in range(0, width, tile):
        total = None
        for e in range(held):
            part = lax.dot_general(
                hidden[:, e * units : (e + 1) * units],
                w_down[e, start : start + tile, :],
                NT,
                preferred_element_type=jnp.float32,
            )
            total = part if total is None else total + part
        total = total.astype(jnp.bfloat16)
        mine[:, start : start + tile] = total[:count]
        for i, other in enumerate(others):
            row = count + i * piece
            other[:, start : start + tile] = total[row : row + piece]


def gated_kernel(*refs, parts):
    inputs, (w_gate, gated, rows) = refs[:parts], refs[parts:]
    held, _, units = w_gate.shape
    weights = gather_inputs(inputs, rows, held)
    for e in range(held):
        gated[:, e * units : (e + 1) * units] = gated_of(rows[...], w_gate[e], weights[e])


def gated_units(parts, w_gate):
    held, width, units = w_gate.shape
    count = sum(rows_in(part, width) for part in parts)
    return pl.pallas_call(
        functools.partial(gated_kernel, parts=len(parts)),
        in_specs=[VMEM_SPEC] * (len(parts) + 1),
        out_specs=[VMEM_SPEC] * 2,
        out_shape=[pltpu.VMEM((count, held * units), jnp.float32), pltpu.VMEM((count, width), jnp.bfloat16)],
        cost_estimate=COST,
        compiler_params=params(),
        name="gated_units",
    )(*in_vmem(*parts, w_gate))


def hidden_kernel(gated, rows, w_up, hidden):
    held, _, units = w_up.shape
    for e in range(held):
        block = slice(e * units, (e + 1) * units)
        up_act = jnp.dot(rows[...], w_up[e], preferred_element_type=jnp.float32)
        hidden[:, block] = (gated[:, block] * up_act).astype(jnp.bfloat16)


def hidden_units(gated, rows, w_up):
    return pl.pallas_call(
        hidden_kernel,
        in_specs=[VMEM_SPEC] * 3,
        out_specs=VMEM_SPEC,
        out_shape=pltpu.VMEM(gated.shape, jnp.bfloat16),
        cost_estimate=COST,
        compiler_params=params(),
        name="hidden_units",
    )(*in_vmem(gated, rows, w_up))


def units_kernel(*refs, parts):
    inputs, (w_gate, w_up), (hidden, rows) = refs[:parts], refs[parts : parts + 2], refs[-2:]
    held, _, units = w_gate.shape
    weights = gather_inputs(inputs, rows, held)
    for e in range(held):
        hidden[:, e * units : (e + 1) * units] = hidden_of(rows[...], w_gate[e], w_up[e], weights[e])


def units_of(parts, w_gate, w_up, *others):
    held, width, units = w_gate.shape
    count = sum(rows_in(part, width) for part in parts)
    return pl.pallas_call(
        functools.partial(units_kernel, parts=len(parts)),
        in_specs=[VMEM_SPEC] * (len(parts) + 2 + len(others)),
        out_specs=VMEM_SPEC,
        out_shape=pltpu.VMEM((count, held * units), jnp.bfloat16),
        scratch_shapes=[pltpu.VMEM((count, width), jnp.bfloat16)],
        cost_estimate=COST,
        compiler_params=params(),
        name="units_of",
    )(*in_vmem(*parts, w_gate, w_up, *others))


def units_sum_kernel(part, w_gate, w_up, mine, twin, hidden, total, rows):
    total[...] = (mine[...].astype(jnp.float32) + twin[...].astype(jnp.float32)).astype(total.dtype)
    held, _, units = w_gate.shape
    weights = gather_inputs([part], rows, held)
    for e in range(held):
        hidden[:, e * units : (e + 1) * units] = hidden_of(rows[...], w_gate[e], w_up[e], weights[e])


def units_and_sum(part, w_gate, w_up, mine, twin):
    held, width, units = w_gate.shape
    count = rows_in(part, width)
    return pl.pallas_call(
        units_sum_kernel,
        in_specs=[VMEM_SPEC] * 5,
        out_specs=[VMEM_SPEC] * 2,
        out_shape=[pltpu.VMEM((count, held * units), jnp.bfloat16), pltpu.VMEM(mine.shape, mine.dtype)],
        scratch_shapes=[pltpu.VMEM((count, width), jnp.bfloat16)],
        cost_estimate=COST,
        compiler_params=params(),
        name="units_and_sum",
    )(*in_vmem(part, w_gate, w_up, mine, twin))


def both_kernel(gated, gated_rows, part, w_gate, w_up, first, second, rows):
    held, _, units = w_gate.shape
    weights = gather_inputs([part], rows, held)
    for e in range(held):
        block = slice(e * units, (e + 1) * units)
        up_act = jnp.dot(gated_rows[...], w_up[e], preferred_element_type=jnp.float32)
        first[:, block] = (gated[:, block] * up_act).astype(jnp.bfloat16)
        second[:, block] = hidden_of(rows[...], w_gate[e], w_up[e], weights[e])


def both_units(gated, gated_rows, part, w_gate, w_up):
    half = pltpu.VMEM(gated.shape, jnp.bfloat16)
    return pl.pallas_call(
        both_kernel,
        in_specs=[VMEM_SPEC] * 5,
        out_specs=[VMEM_SPEC] * 2,
        out_shape=[half, half],
        scratch_shapes=[pltpu.VMEM(gated_rows.shape, jnp.bfloat16)],
        cost_estimate=COST,
        compiler_params=params(),
        name="both_units",
    )(*in_vmem(gated, gated_rows, part, w_gate, w_up))


def rest_kernel(first, part, w_gate, w_up, w_down, mine, other, rows, hidden):
    held, _, units = w_gate.shape
    count = first.shape[0]
    weights = gather_inputs([part], rows, held)
    for e in range(held):
        block = slice(e * units, (e + 1) * units)
        hidden[:count, block] = first[:, block]
        hidden[count:, block] = hidden_of(rows[...], w_gate[e], w_up[e], weights[e])
    down_all(hidden, w_down, mine, other)


def rest_of(first, part, w_gate, w_up, w_down):
    held, width, units = w_gate.shape
    count = rows_in(part, width)
    return pl.pallas_call(
        rest_kernel,
        in_specs=[VMEM_SPEC] * 5,
        out_specs=[VMEM_SPEC] * 2,
        out_shape=[pltpu.VMEM((count, width), jnp.bfloat16)] * 2,
        scratch_shapes=[
            pltpu.VMEM((count, width), jnp.bfloat16),
            pltpu.VMEM((2 * count, held * units), jnp.bfloat16),
        ],
        cost_estimate=COST,
        compiler_params=params(),
        name="rest_of",
    )(*in_vmem(first, part, w_gate, w_up, w_down))


def sums_kernel(first, second, w_down, mine, *refs):
    *others, hidden = refs
    count = first.shape[0]
    hidden[:count] = first[...]
    hidden[count:] = second[...]
    down_all(hidden, w_down, mine, *others)


def sums_of(first, second, w_down, pieces=1):
    count, width = first.shape[0], w_down.shape[1]
    others = [pltpu.VMEM((count // pieces, width), jnp.bfloat16)] * pieces
    return pl.pallas_call(
        sums_kernel,
        in_specs=[VMEM_SPEC] * 3,
        out_specs=[VMEM_SPEC] * (1 + pieces),
        out_shape=[pltpu.VMEM((count, width), jnp.bfloat16), *others],
        scratch_shapes=[pltpu.VMEM((2 * count, first.shape[1]), jnp.bfloat16)],
        cost_estimate=COST,
        compiler_params=params(),
        name="sums_of",
    )(*in_vmem(first, second, w_down))


def pieces_kernel(mine, *refs):
    *others, out = refs
    piece = others[0].shape[0]
    for i, other in enumerate(others):
        rows = slice(i * piece, (i + 1) * piece)
        out[rows] = (mine[rows].astype(jnp.float32) + other[...].astype(jnp.float32)).astype(out.dtype)


def add_pieces(mine, others):
    return pl.pallas_call(
        pieces_kernel,
        in_specs=[VMEM_SPEC] * (1 + len(others)),
        out_specs=VMEM_SPEC,
        out_shape=pltpu.VMEM(mine.shape, mine.dtype),
        cost_estimate=COST,
        compiler_params=params(8),
        name="add_pieces",
    )(*in_vmem(mine, *others))


def down_units(hidden, w_down, pieces=1):
    count, width = hidden.shape[0] // 2, w_down.shape[1]
    others = [pltpu.VMEM((count // pieces, width), jnp.bfloat16)] * pieces
    return pl.pallas_call(
        down_all,
        in_specs=[VMEM_SPEC] * 2,
        out_specs=[VMEM_SPEC] * (1 + pieces),
        out_shape=[pltpu.VMEM((count, width), jnp.bfloat16), *others],
        cost_estimate=COST,
        compiler_params=params(),
        name="down_units",
    )(*in_vmem(hidden, w_down))


def add_kernel(*refs):
    *parts, out = refs
    width = parts[0].shape[1]
    total = parts[0][...].astype(jnp.float32)
    for part in parts[1:]:
        total += part[:, :width].astype(jnp.float32)
    out[:, :width] = total.astype(out.dtype)
    if out.shape[1] > width:
        out[:, width:] = jnp.zeros((out.shape[0], out.shape[1] - width), out.dtype)


def add(*parts, dtype=jnp.bfloat16, spare=0, cost=COST):
    count, width = parts[0].shape
    return pl.pallas_call(
        add_kernel,
        in_specs=[VMEM_SPEC] * len(parts),
        out_specs=VMEM_SPEC,
        out_shape=pltpu.VMEM((count, width + spare), dtype),
        cost_estimate=cost,
        compiler_params=params(8),
        name="add",
    )(*in_vmem(*parts))


def finish_kernel(*refs, pieces):
    *parts, out, block, sems = refs
    twins, parts = parts[:pieces], parts[pieces:]
    count = block.shape[1]
    copies = []
    for i in range(block.shape[0]):
        start = i * count
        rows = pl.ds(start, count)
        size = twins[0].shape[0]
        total = twins[start // size][pl.ds(start % size, count)].astype(jnp.float32)
        for part in parts:
            total += part[rows].astype(jnp.float32)
        block[i] = total.astype(block.dtype)
        copies.append(pltpu.make_async_copy(block.at[i], out.at[rows], sems.at[i]))
        copies[-1].start()
    for copy in copies:
        copy.wait()


def finish(twins, *parts, blocks=4):
    count, width = parts[0].shape
    return pl.pallas_call(
        functools.partial(finish_kernel, pieces=len(twins)),
        in_specs=[VMEM_SPEC] * (len(twins) + len(parts)),
        out_specs=HBM_SPEC,
        out_shape=jax.ShapeDtypeStruct((count, width), jnp.bfloat16),
        scratch_shapes=[
            pltpu.VMEM((blocks, count // blocks, width), jnp.bfloat16),
            pltpu.SemaphoreType.DMA((blocks,)),
        ],
        cost_estimate=COST,
        compiler_params=params(8),
        name="finish",
    )(*in_vmem(*twins, *parts))


def on_four_chips(tokens, low, high, table, w_gate, w_up, w_down):
    x, y = 2, 4
    barrier = lax.optimization_barrier
    weights = (w_gate, w_up, w_down)
    near_rows, near_table = cross(tokens, x, y), cross(table, x, y)
    gated, rows = gated_units([low, high, flip(low, CORE), flip(high, CORE)], w_gate)
    wide = join(low, high, table, tokens.shape[1], SPARE)
    near_table, near_rows, gated, wide = barrier((near_table, near_rows, gated, wide))
    near = pack(near_rows, near_table)

    far = cross(near, y, x)
    mine_near, other_near = rest_of(units_of([near], *weights), flip(near, CORE), *weights)
    following = cross(wide, y, x)
    far, mine_near = barrier((far, mine_near))

    far_twin = flip(far, CORE)
    first = units_of([far], w_gate, w_up)
    first, far_twin = barrier((first, far_twin))
    second, sum_near = units_and_sum(far_twin, w_gate, w_up, mine_near, flip(other_near, CORE))
    back = cross(sum_near, x, y)
    following, second = barrier((following, second))
    mine_far, *other_far = sums_of(first, second, w_down, pieces=2)

    following_twin = flip(following, CORE)
    first, first_rows = gated_units([following], w_gate)
    mine_far, first = barrier((mine_far, first))
    sum_far = add_pieces(mine_far, [flip(other, CORE) for other in other_far])
    sum_far, following_twin, first = barrier((sum_far, following_twin, first))
    relay = cross(sum_far, x, y)
    first, second = both_units(first, first_rows, following_twin, w_gate, w_up)
    second, back = barrier((second, back))
    mine_last, other_last = sums_of(first, second, w_down)
    sum_last = add(add(mine_last, relay, dtype=jnp.float32, cost=RELAY), flip(other_last, CORE))
    last = cross(sum_last, y, x)
    hidden = hidden_units(gated, rows, w_up)
    mine_own, *other_own = down_units(hidden, w_down, pieces=2)
    return finish([flip(other, CORE) for other in other_own], mine_own, back, last)


def on_any_chips(tokens, low, high, table, *weights):
    own = join(low, high, table, tokens.shape[1])
    offsets = range(2, lax.axis_size("ep"), 2)
    arrived = [flip(own, d) for d in offsets]
    parts = []
    for d, rows in zip([0, *offsets], [own, *arrived]):
        mine, other = rest_of(units_of([rows], *weights[:2]), flip(rows, CORE), *weights)
        other = flip(other, CORE)
        parts += [flip(add(mine, other), d)] if d else [mine, other]
    return finish(parts[:1], *parts[1:])


def body(tokens, experts, gates, w_gate, w_up, w_down):
    n_ep = lax.axis_size("ep")
    n_experts = w_gate.shape[0] * n_ep
    packed = prepare(tokens, experts, gates, n_experts)
    run = on_four_chips if n_ep == 8 else on_any_chips
    return run(tokens, *packed, w_gate, w_up, w_down)


def solution(mesh):
    in_specs = (
        P(("rep", "ep"), None),
        P(("rep", "ep"), None),
        P(("rep", "ep"), None),
        P("ep", None, None),
        P("ep", None, None),
        P("ep", None, None),
    )
    out_specs = P(("rep", "ep"), None)
    return jax.shard_map(body, mesh=mesh, in_specs=in_specs, out_specs=out_specs, check_vma=False)
```

```python
import functools

import jax
import jax.numpy as jnp
from jax import lax
from jax.experimental import pallas as pl
from jax.experimental.pallas import tpu as pltpu
from jax.sharding import PartitionSpec as P

MIB = 2**20
LANES = 128
NT = (((1,), (1,)), ((), ()))
VMEM_SPEC = pl.BlockSpec(memory_space=pltpu.VMEM)
HBM_SPEC = pl.BlockSpec(memory_space=pltpu.HBM)
CORE = 1
PACK = 16
SPARE = LANES
MEDIUM = pl.CostEstimate(flops=0, bytes_accessed=3 * 10**6, transcendentals=0)
RELAY = pl.CostEstimate(flops=2 * 10**8, bytes_accessed=3 * 10**6, transcendentals=0)
LONG = pl.CostEstimate(flops=10**11, bytes_accessed=10**8, transcendentals=0)
COST = pl.CostEstimate(flops=0, bytes_accessed=0, transcendentals=0)


def flip(x, mask):
    n = lax.axis_size("ep")
    return lax.ppermute(x, "ep", [(i, i ^ mask) for i in range(n)])


def cross(x, even, odd):
    n = lax.axis_size("ep")
    return lax.ppermute(x, "ep", [(i, i ^ (odd if i % 2 else even)) for i in range(n)])


def in_vmem(*arrays):
    return [pltpu.with_memory_space_constraint(a, pltpu.VMEM) for a in arrays]


def in_hbm(*arrays):
    return [pltpu.with_memory_space_constraint(a, pltpu.HBM) for a in arrays]


def params(limit=6):
    return pltpu.CompilerParams(vmem_limit_bytes=limit * MIB)


def prepare_kernel(tokens, experts, gates, low, high, table, chosen, weight, sems, *, n_experts):
    count, width = tokens.shape
    groups = count // PACK
    half = groups // 2
    copies = [
        pltpu.make_async_copy(experts, chosen, sems.at[0]),
        pltpu.make_async_copy(gates, weight, sems.at[1]),
    ]
    for j in range(groups):
        rows = tokens.at[pl.ds(j * PACK, PACK)]
        place = (low if j < half else high).at[:, pl.ds(j % half * width, width)]
        copies.append(pltpu.make_async_copy(rows, place, sems.at[2 + j]))
    for copy in copies:
        copy.start()
    copies[0].wait()
    copies[1].wait()
    ids = lax.broadcasted_iota(jnp.int32, (-(-n_experts // LANES) * LANES, count), 0)
    total = jnp.zeros(ids.shape, jnp.float32)
    for k in range(chosen.shape[0]):
        gate = weight[k : k + 1, :].astype(jnp.float32)
        total += jnp.where(ids == chosen[k : k + 1, :], gate, 0.0)
    total = total.T
    blocks = [total[j * PACK : (j + 1) * PACK, :n_experts] for j in range(groups)]
    for out, first, last in ((low, 0, half), (high, half, groups), (table, 0, groups)):
        start = 0 if out is table else half * width
        spare = out.shape[1] - start - (last - first) * n_experts
        values = blocks[first:last] + ([jnp.zeros((PACK, spare), jnp.float32)] if spare else [])
        out[:, start:] = jnp.concatenate(values, axis=1).astype(jnp.bfloat16)
    for copy in copies[2:]:
        copy.wait()


def table_lanes(groups, n_experts):
    return -(-groups * n_experts // LANES) * LANES


def prepare(tokens, experts, gates, n_experts):
    count, width = tokens.shape
    groups = count // PACK
    half = groups // 2 * width + table_lanes(groups // 2, n_experts)
    lanes = [half, half, table_lanes(groups, n_experts)]
    return pl.pallas_call(
        functools.partial(prepare_kernel, n_experts=n_experts),
        in_specs=[HBM_SPEC] * 3,
        out_specs=[VMEM_SPEC] * 3,
        out_shape=[pltpu.VMEM((PACK, size), jnp.bfloat16) for size in lanes],
        scratch_shapes=[
            pltpu.VMEM(experts.shape[::-1], jnp.int32),
            pltpu.VMEM(gates.shape[::-1], jnp.bfloat16),
            pltpu.SemaphoreType.DMA((2 + groups,)),
        ],
        cost_estimate=LONG,
        compiler_params=params(4),
        name="prepare",
    )(*in_hbm(tokens, experts.T, gates.T))


def join_kernel(low, high, table, out, *, width):
    part = low.shape[1] // width * width
    out[:, :part] = low[:, :part]
    out[:, part : 2 * part] = high[:, :part]
    out[:, 2 * part : 2 * part + table.shape[1]] = table[...]
    if out.shape[1] > 2 * part + table.shape[1]:
        spare = out.shape[1] - 2 * part - table.shape[1]
        out[:, 2 * part + table.shape[1] :] = jnp.zeros((PACK, spare), out.dtype)


def join(low, high, table, width, spare=0):
    lanes = low.shape[1] // width * width * 2 + table.shape[1] + spare
    return pl.pallas_call(
        functools.partial(join_kernel, width=width),
        in_specs=[VMEM_SPEC] * 3,
        out_specs=VMEM_SPEC,
        out_shape=pltpu.VMEM((PACK, lanes), low.dtype),
        cost_estimate=COST,
        compiler_params=params(4),
        name="join",
    )(*in_vmem(low, high, table))


def pack_kernel(rows, table, out):
    width = rows.shape[1]
    for j in range(rows.shape[0] // PACK):
        out[:, j * width : (j + 1) * width] = rows[j * PACK : (j + 1) * PACK]
    out[:, rows.shape[0] // PACK * width :] = table[...]


def pack(rows, table):
    return pl.pallas_call(
        pack_kernel,
        in_specs=[VMEM_SPEC] * 2,
        out_specs=VMEM_SPEC,
        out_shape=pltpu.VMEM((PACK, rows.size // PACK + table.shape[1]), rows.dtype),
        cost_estimate=COST,
        compiler_params=params(4),
        name="pack",
    )(*in_vmem(rows, table))


def rows_in(part, width):
    return part.shape[1] // width * PACK


def gather_inputs(parts, rows, held):
    width = rows.shape[1]
    n_experts = held * lax.axis_size("ep")
    base = lax.axis_index("ep") * held
    columns = [[] for _ in range(held)]
    start = 0
    for part in parts:
        groups = part.shape[1] // width
        table = part[:, groups * width :].astype(jnp.float32)
        lane = lax.broadcasted_iota(jnp.int32, table.shape, 1)
        for j in range(groups):
            rows[start : start + PACK] = part[:, j * width : (j + 1) * width]
            start += PACK
            for e in range(held):
                gate = jnp.where(lane == j * n_experts + base + e, table, 0.0)
                columns[e].append(jnp.sum(gate, axis=1, keepdims=True))
    return [jnp.concatenate(column, axis=0) for column in columns]


def gated_of(rows, gate_w, weight):
    gate_act = jnp.dot(rows, gate_w, preferred_element_type=jnp.float32)
    return gate_act * (0.5 * jnp.tanh(0.5 * gate_act) + 0.5) * weight


def hidden_of(rows, gate_w, up_w, weight):
    up_act = jnp.dot(rows, up_w, preferred_element_type=jnp.float32)
    return (gated_of(rows, gate_w, weight) * up_act).astype(jnp.bfloat16)


def down_all(hidden, w_down, mine, *others, tile=512):
    held, width, units = w_down.shape
    count, piece = mine.shape[0], others[0].shape[0]
    for start in range(0, width, tile):
        total = None
        for e in range(held):
            part = lax.dot_general(
                hidden[:, e * units : (e + 1) * units],
                w_down[e, start : start + tile, :],
                NT,
                preferred_element_type=jnp.float32,
            )
            total = part if total is None else total + part
        total = total.astype(jnp.bfloat16)
        mine[:, start : start + tile] = total[:count]
        for i, other in enumerate(others):
            row = count + i * piece
            other[:, start : start + tile] = total[row : row + piece]


def gated_kernel(*refs, parts):
    inputs, (w_gate, gated, rows) = refs[:parts], refs[parts:]
    held, _, units = w_gate.shape
    weights = gather_inputs(inputs, rows, held)
    for e in range(held):
        gated[:, e * units : (e + 1) * units] = gated_of(rows[...], w_gate[e], weights[e])


def gated_units(parts, w_gate):
    held, width, units = w_gate.shape
    count = sum(rows_in(part, width) for part in parts)
    return pl.pallas_call(
        functools.partial(gated_kernel, parts=len(parts)),
        in_specs=[VMEM_SPEC] * (len(parts) + 1),
        out_specs=[VMEM_SPEC] * 2,
        out_shape=[pltpu.VMEM((count, held * units), jnp.float32), pltpu.VMEM((count, width), jnp.bfloat16)],
        cost_estimate=COST,
        compiler_params=params(),
        name="gated_units",
    )(*in_vmem(*parts, w_gate))


def hidden_kernel(gated, rows, w_up, hidden):
    held, _, units = w_up.shape
    for e in range(held):
        block = slice(e * units, (e + 1) * units)
        up_act = jnp.dot(rows[...], w_up[e], preferred_element_type=jnp.float32)
        hidden[:, block] = (gated[:, block] * up_act).astype(jnp.bfloat16)


def hidden_units(gated, rows, w_up):
    return pl.pallas_call(
        hidden_kernel,
        in_specs=[VMEM_SPEC] * 3,
        out_specs=VMEM_SPEC,
        out_shape=pltpu.VMEM(gated.shape, jnp.bfloat16),
        cost_estimate=COST,
        compiler_params=params(),
        name="hidden_units",
    )(*in_vmem(gated, rows, w_up))


def units_kernel(*refs, parts):
    inputs, (w_gate, w_up), (hidden, rows) = refs[:parts], refs[parts : parts + 2], refs[-2:]
    held, _, units = w_gate.shape
    weights = gather_inputs(inputs, rows, held)
    for e in range(held):
        hidden[:, e * units : (e + 1) * units] = hidden_of(rows[...], w_gate[e], w_up[e], weights[e])


def units_of(parts, w_gate, w_up, *others):
    held, width, units = w_gate.shape
    count = sum(rows_in(part, width) for part in parts)
    return pl.pallas_call(
        functools.partial(units_kernel, parts=len(parts)),
        in_specs=[VMEM_SPEC] * (len(parts) + 2 + len(others)),
        out_specs=VMEM_SPEC,
        out_shape=pltpu.VMEM((count, held * units), jnp.bfloat16),
        scratch_shapes=[pltpu.VMEM((count, width), jnp.bfloat16)],
        cost_estimate=COST,
        compiler_params=params(),
        name="units_of",
    )(*in_vmem(*parts, w_gate, w_up, *others))


def both_kernel(gated, gated_rows, part, w_gate, w_up, first, second, rows):
    held, _, units = w_gate.shape
    weights = gather_inputs([part], rows, held)
    for e in range(held):
        block = slice(e * units, (e + 1) * units)
        up_act = jnp.dot(gated_rows[...], w_up[e], preferred_element_type=jnp.float32)
        first[:, block] = (gated[:, block] * up_act).astype(jnp.bfloat16)
        second[:, block] = hidden_of(rows[...], w_gate[e], w_up[e], weights[e])


def both_units(gated, gated_rows, part, w_gate, w_up):
    half = pltpu.VMEM(gated.shape, jnp.bfloat16)
    return pl.pallas_call(
        both_kernel,
        in_specs=[VMEM_SPEC] * 5,
        out_specs=[VMEM_SPEC] * 2,
        out_shape=[half, half],
        scratch_shapes=[pltpu.VMEM(gated_rows.shape, jnp.bfloat16)],
        cost_estimate=COST,
        compiler_params=params(),
        name="both_units",
    )(*in_vmem(gated, gated_rows, part, w_gate, w_up))


def rest_kernel(first, part, w_gate, w_up, w_down, mine, other, rows, hidden):
    held, _, units = w_gate.shape
    count = first.shape[0]
    weights = gather_inputs([part], rows, held)
    for e in range(held):
        block = slice(e * units, (e + 1) * units)
        hidden[:count, block] = first[:, block]
        hidden[count:, block] = hidden_of(rows[...], w_gate[e], w_up[e], weights[e])
    down_all(hidden, w_down, mine, other)


def rest_of(first, part, w_gate, w_up, w_down):
    held, width, units = w_gate.shape
    count = rows_in(part, width)
    return pl.pallas_call(
        rest_kernel,
        in_specs=[VMEM_SPEC] * 5,
        out_specs=[VMEM_SPEC] * 2,
        out_shape=[pltpu.VMEM((count, width), jnp.bfloat16)] * 2,
        scratch_shapes=[
            pltpu.VMEM((count, width), jnp.bfloat16),
            pltpu.VMEM((2 * count, held * units), jnp.bfloat16),
        ],
        cost_estimate=COST,
        compiler_params=params(),
        name="rest_of",
    )(*in_vmem(first, part, w_gate, w_up, w_down))


def sums_kernel(first, second, w_down, mine, *refs):
    *others, hidden = refs
    count = first.shape[0]
    hidden[:count] = first[...]
    hidden[count:] = second[...]
    down_all(hidden, w_down, mine, *others)


def sums_of(first, second, w_down, pieces=1):
    count, width = first.shape[0], w_down.shape[1]
    others = [pltpu.VMEM((count // pieces, width), jnp.bfloat16)] * pieces
    return pl.pallas_call(
        sums_kernel,
        in_specs=[VMEM_SPEC] * 3,
        out_specs=[VMEM_SPEC] * (1 + pieces),
        out_shape=[pltpu.VMEM((count, width), jnp.bfloat16), *others],
        scratch_shapes=[pltpu.VMEM((2 * count, first.shape[1]), jnp.bfloat16)],
        cost_estimate=COST,
        compiler_params=params(),
        name="sums_of",
    )(*in_vmem(first, second, w_down))


def pieces_kernel(mine, *refs):
    *others, out = refs
    piece = others[0].shape[0]
    for i, other in enumerate(others):
        rows = slice(i * piece, (i + 1) * piece)
        out[rows] = (mine[rows].astype(jnp.float32) + other[...].astype(jnp.float32)).astype(out.dtype)


def add_pieces(mine, others):
    return pl.pallas_call(
        pieces_kernel,
        in_specs=[VMEM_SPEC] * (1 + len(others)),
        out_specs=VMEM_SPEC,
        out_shape=pltpu.VMEM(mine.shape, mine.dtype),
        cost_estimate=COST,
        compiler_params=params(8),
        name="add_pieces",
    )(*in_vmem(mine, *others))


def down_units(hidden, w_down, pieces=1):
    count, width = hidden.shape[0] // 2, w_down.shape[1]
    others = [pltpu.VMEM((count // pieces, width), jnp.bfloat16)] * pieces
    return pl.pallas_call(
        down_all,
        in_specs=[VMEM_SPEC] * 2,
        out_specs=[VMEM_SPEC] * (1 + pieces),
        out_shape=[pltpu.VMEM((count, width), jnp.bfloat16), *others],
        cost_estimate=COST,
        compiler_params=params(),
        name="down_units",
    )(*in_vmem(hidden, w_down))


def add_kernel(*refs):
    *parts, out = refs
    width = parts[0].shape[1]
    total = parts[0][...].astype(jnp.float32)
    for part in parts[1:]:
        total += part[:, :width].astype(jnp.float32)
    out[:, :width] = total.astype(out.dtype)
    if out.shape[1] > width:
        out[:, width:] = jnp.zeros((out.shape[0], out.shape[1] - width), out.dtype)


def add(*parts, dtype=jnp.bfloat16, spare=0, cost=COST):
    count, width = parts[0].shape
    return pl.pallas_call(
        add_kernel,
        in_specs=[VMEM_SPEC] * len(parts),
        out_specs=VMEM_SPEC,
        out_shape=pltpu.VMEM((count, width + spare), dtype),
        cost_estimate=cost,
        compiler_params=params(8),
        name="add",
    )(*in_vmem(*parts))


def finish_kernel(*refs, pieces):
    *parts, out, block, sems = refs
    twins, parts = parts[:pieces], parts[pieces:]
    count = block.shape[1]
    copies = []
    for i in range(block.shape[0]):
        start = i * count
        rows = pl.ds(start, count)
        size = twins[0].shape[0]
        total = twins[start // size][pl.ds(start % size, count)].astype(jnp.float32)
        for part in parts:
            total += part[rows, : block.shape[2]].astype(jnp.float32)
        block[i] = total.astype(block.dtype)
        copies.append(pltpu.make_async_copy(block.at[i], out.at[rows], sems.at[i]))
        copies[-1].start()
    for copy in copies:
        copy.wait()


def finish(twins, *parts, blocks=4):
    count, width = parts[0].shape
    return pl.pallas_call(
        functools.partial(finish_kernel, pieces=len(twins)),
        in_specs=[VMEM_SPEC] * (len(twins) + len(parts)),
        out_specs=HBM_SPEC,
        out_shape=jax.ShapeDtypeStruct((count, width), jnp.bfloat16),
        scratch_shapes=[
            pltpu.VMEM((blocks, count // blocks, width), jnp.bfloat16),
            pltpu.SemaphoreType.DMA((blocks,)),
        ],
        cost_estimate=COST,
        compiler_params=params(8),
        name="finish",
    )(*in_vmem(*twins, *parts))


def on_four_chips(tokens, low, high, table, w_gate, w_up, w_down):
    x, y = 2, 4
    barrier = lax.optimization_barrier
    weights = (w_gate, w_up, w_down)
    near_rows, near_table = cross(tokens, x, y), cross(table, x, y)
    gated, rows = gated_units([low, high, flip(low, CORE), flip(high, CORE)], w_gate)
    near_table, near_rows, gated = barrier((near_table, near_rows, gated))
    near = pack(near_rows, near_table)

    far = cross(near, y, x)
    mine_near, other_near = rest_of(units_of([near], *weights), flip(near, CORE), *weights)
    following = cross(join(low, high, table, tokens.shape[1], SPARE), y, x)
    far, mine_near = barrier((far, mine_near))

    far_twin = flip(far, CORE)
    first = units_of([far], w_gate, w_up)
    first, far_twin = barrier((first, far_twin))
    second = units_of([far_twin], w_gate, w_up)
    mine_near, second = barrier((mine_near, second))
    sum_near = add(mine_near, flip(other_near, CORE), spare=LANES)
    back = cross(sum_near, x, y)
    following, second = barrier((following, second))
    mine_far, *other_far = sums_of(first, second, w_down)

    following_twin = flip(following, CORE)
    first, first_rows = gated_units([following], w_gate)
    mine_far, first = barrier((mine_far, first))
    sum_far = add_pieces(mine_far, [flip(other, CORE) for other in other_far])
    sum_far, following_twin, first = barrier((sum_far, following_twin, first))
    relay = cross(sum_far, x, y)
    first, second = both_units(first, first_rows, following_twin, w_gate, w_up)
    second, back = barrier((second, back))
    mine_last, other_last = sums_of(first, second, w_down)
    sum_last = add(add(mine_last, relay, dtype=jnp.float32, cost=RELAY), flip(other_last, CORE))
    last = cross(sum_last, y, x)
    hidden = hidden_units(gated, rows, w_up)
    mine_own, *other_own = down_units(hidden, w_down, pieces=2)
    return finish([flip(other, CORE) for other in other_own], mine_own, back, last)


def on_any_chips(tokens, low, high, table, *weights):
    own = join(low, high, table, tokens.shape[1])
    offsets = range(2, lax.axis_size("ep"), 2)
    arrived = [flip(own, d) for d in offsets]
    parts = []
    for d, rows in zip([0, *offsets], [own, *arrived]):
        mine, other = rest_of(units_of([rows], *weights[:2]), flip(rows, CORE), *weights)
        other = flip(other, CORE)
        parts += [flip(add(mine, other), d)] if d else [mine, other]
    return finish(parts[:1], *parts[1:])


def body(tokens, experts, gates, w_gate, w_up, w_down):
    n_ep = lax.axis_size("ep")
    n_experts = w_gate.shape[0] * n_ep
    packed = prepare(tokens, experts, gates, n_experts)
    run = on_four_chips if n_ep == 8 else on_any_chips
    return run(tokens, *packed, w_gate, w_up, w_down)


def solution(mesh):
    in_specs = (
        P(("rep", "ep"), None),
        P(("rep", "ep"), None),
        P(("rep", "ep"), None),
        P("ep", None, None),
        P("ep", None, None),
        P("ep", None, None),
    )
    out_specs = P(("rep", "ep"), None)
    return jax.shard_map(body, mesh=mesh, in_specs=in_specs, out_specs=out_specs, check_vma=False)
```

```python
import functools

import jax
import jax.numpy as jnp
from jax import lax
from jax.experimental import pallas as pl
from jax.experimental.pallas import tpu as pltpu
from jax.sharding import PartitionSpec as P

MIB = 2**20
LANES = 128
NT = (((1,), (1,)), ((), ()))
VMEM_SPEC = pl.BlockSpec(memory_space=pltpu.VMEM)
HBM_SPEC = pl.BlockSpec(memory_space=pltpu.HBM)
CORE = 1
PACK = 16
SPARE = LANES
MEDIUM = pl.CostEstimate(flops=0, bytes_accessed=3 * 10**6, transcendentals=0)
RELAY = pl.CostEstimate(flops=2 * 10**8, bytes_accessed=3 * 10**6, transcendentals=0)
LONG = pl.CostEstimate(flops=10**11, bytes_accessed=10**8, transcendentals=0)
COST = pl.CostEstimate(flops=0, bytes_accessed=0, transcendentals=0)


def flip(x, mask):
    n = lax.axis_size("ep")
    return lax.ppermute(x, "ep", [(i, i ^ mask) for i in range(n)])


def cross(x, even, odd):
    n = lax.axis_size("ep")
    return lax.ppermute(x, "ep", [(i, i ^ (odd if i % 2 else even)) for i in range(n)])


def in_vmem(*arrays):
    return [pltpu.with_memory_space_constraint(a, pltpu.VMEM) for a in arrays]


def in_hbm(*arrays):
    return [pltpu.with_memory_space_constraint(a, pltpu.HBM) for a in arrays]


def params(limit=6):
    return pltpu.CompilerParams(vmem_limit_bytes=limit * MIB)


def prepare_kernel(tokens, experts, gates, low, high, table, chosen, weight, sems, *, n_experts):
    count, width = tokens.shape
    groups = count // PACK
    half = groups // 2
    copies = [
        pltpu.make_async_copy(experts, chosen, sems.at[0]),
        pltpu.make_async_copy(gates, weight, sems.at[1]),
    ]
    for j in range(groups):
        rows = tokens.at[pl.ds(j * PACK, PACK)]
        place = (low if j < half else high).at[:, pl.ds(j % half * width, width)]
        copies.append(pltpu.make_async_copy(rows, place, sems.at[2 + j]))
    for copy in copies:
        copy.start()
    copies[0].wait()
    copies[1].wait()
    ids = lax.broadcasted_iota(jnp.int32, (-(-n_experts // LANES) * LANES, count), 0)
    total = jnp.zeros(ids.shape, jnp.float32)
    for k in range(chosen.shape[0]):
        gate = weight[k : k + 1, :].astype(jnp.float32)
        total += jnp.where(ids == chosen[k : k + 1, :], gate, 0.0)
    total = total.T
    blocks = [total[j * PACK : (j + 1) * PACK, :n_experts] for j in range(groups)]
    for out, first, last in ((low, 0, half), (high, half, groups), (table, 0, groups)):
        start = 0 if out is table else half * width
        spare = out.shape[1] - start - (last - first) * n_experts
        values = blocks[first:last] + ([jnp.zeros((PACK, spare), jnp.float32)] if spare else [])
        out[:, start:] = jnp.concatenate(values, axis=1).astype(jnp.bfloat16)
    for copy in copies[2:]:
        copy.wait()


def table_lanes(groups, n_experts):
    return -(-groups * n_experts // LANES) * LANES


def prepare(tokens, experts, gates, n_experts):
    count, width = tokens.shape
    groups = count // PACK
    half = groups // 2 * width + table_lanes(groups // 2, n_experts)
    lanes = [half, half, table_lanes(groups, n_experts)]
    return pl.pallas_call(
        functools.partial(prepare_kernel, n_experts=n_experts),
        in_specs=[HBM_SPEC] * 3,
        out_specs=[VMEM_SPEC] * 3,
        out_shape=[pltpu.VMEM((PACK, size), jnp.bfloat16) for size in lanes],
        scratch_shapes=[
            pltpu.VMEM(experts.shape[::-1], jnp.int32),
            pltpu.VMEM(gates.shape[::-1], jnp.bfloat16),
            pltpu.SemaphoreType.DMA((2 + groups,)),
        ],
        cost_estimate=LONG,
        compiler_params=params(4),
        name="prepare",
    )(*in_hbm(tokens, experts.T, gates.T))


def join_kernel(low, high, table, out, *, width):
    part = low.shape[1] // width * width
    out[:, :part] = low[:, :part]
    out[:, part : 2 * part] = high[:, :part]
    out[:, 2 * part : 2 * part + table.shape[1]] = table[...]
    if out.shape[1] > 2 * part + table.shape[1]:
        spare = out.shape[1] - 2 * part - table.shape[1]
        out[:, 2 * part + table.shape[1] :] = jnp.zeros((PACK, spare), out.dtype)


def join(low, high, table, width, spare=0):
    lanes = low.shape[1] // width * width * 2 + table.shape[1] + spare
    return pl.pallas_call(
        functools.partial(join_kernel, width=width),
        in_specs=[VMEM_SPEC] * 3,
        out_specs=VMEM_SPEC,
        out_shape=pltpu.VMEM((PACK, lanes), low.dtype),
        cost_estimate=COST,
        compiler_params=params(4),
        name="join",
    )(*in_vmem(low, high, table))


def pack_kernel(rows, table, out):
    width = rows.shape[1]
    for j in range(rows.shape[0] // PACK):
        out[:, j * width : (j + 1) * width] = rows[j * PACK : (j + 1) * PACK]
    out[:, rows.shape[0] // PACK * width :] = table[...]


def pack(rows, table):
    return pl.pallas_call(
        pack_kernel,
        in_specs=[VMEM_SPEC] * 2,
        out_specs=VMEM_SPEC,
        out_shape=pltpu.VMEM((PACK, rows.size // PACK + table.shape[1]), rows.dtype),
        cost_estimate=COST,
        compiler_params=params(4),
        name="pack",
    )(*in_vmem(rows, table))


def rows_in(part, width):
    return part.shape[1] // width * PACK


def gather_inputs(parts, rows, held):
    width = rows.shape[1]
    n_experts = held * lax.axis_size("ep")
    base = lax.axis_index("ep") * held
    columns = [[] for _ in range(held)]
    start = 0
    for part in parts:
        groups = part.shape[1] // width
        table = part[:, groups * width :].astype(jnp.float32)
        lane = lax.broadcasted_iota(jnp.int32, table.shape, 1)
        for j in range(groups):
            rows[start : start + PACK] = part[:, j * width : (j + 1) * width]
            start += PACK
            for e in range(held):
                gate = jnp.where(lane == j * n_experts + base + e, table, 0.0)
                columns[e].append(jnp.sum(gate, axis=1, keepdims=True))
    return [jnp.concatenate(column, axis=0) for column in columns]


def gated_of(rows, gate_w, weight):
    gate_act = jnp.dot(rows, gate_w, preferred_element_type=jnp.float32)
    return gate_act * (0.5 * jnp.tanh(0.5 * gate_act) + 0.5) * weight


def hidden_of(rows, gate_w, up_w, weight):
    up_act = jnp.dot(rows, up_w, preferred_element_type=jnp.float32)
    return (gated_of(rows, gate_w, weight) * up_act).astype(jnp.bfloat16)


def down_all(hidden, w_down, mine, *others, tile=512):
    held, width, units = w_down.shape
    count, piece = mine.shape[0], others[0].shape[0]
    for start in range(0, width, tile):
        total = None
        for e in range(held):
            part = lax.dot_general(
                hidden[:, e * units : (e + 1) * units],
                w_down[e, start : start + tile, :],
                NT,
                preferred_element_type=jnp.float32,
            )
            total = part if total is None else total + part
        total = total.astype(jnp.bfloat16)
        mine[:, start : start + tile] = total[:count]
        for i, other in enumerate(others):
            row = count + i * piece
            other[:, start : start + tile] = total[row : row + piece]


def gated_kernel(*refs, parts):
    inputs, (w_gate, gated, rows) = refs[:parts], refs[parts:]
    held, _, units = w_gate.shape
    weights = gather_inputs(inputs, rows, held)
    for e in range(held):
        gated[:, e * units : (e + 1) * units] = gated_of(rows[...], w_gate[e], weights[e])


def gated_units(parts, w_gate):
    held, width, units = w_gate.shape
    count = sum(rows_in(part, width) for part in parts)
    return pl.pallas_call(
        functools.partial(gated_kernel, parts=len(parts)),
        in_specs=[VMEM_SPEC] * (len(parts) + 1),
        out_specs=[VMEM_SPEC] * 2,
        out_shape=[pltpu.VMEM((count, held * units), jnp.float32), pltpu.VMEM((count, width), jnp.bfloat16)],
        cost_estimate=COST,
        compiler_params=params(),
        name="gated_units",
    )(*in_vmem(*parts, w_gate))


def hidden_kernel(gated, rows, w_up, hidden):
    held, _, units = w_up.shape
    for e in range(held):
        block = slice(e * units, (e + 1) * units)
        up_act = jnp.dot(rows[...], w_up[e], preferred_element_type=jnp.float32)
        hidden[:, block] = (gated[:, block] * up_act).astype(jnp.bfloat16)


def hidden_units(gated, rows, w_up):
    return pl.pallas_call(
        hidden_kernel,
        in_specs=[VMEM_SPEC] * 3,
        out_specs=VMEM_SPEC,
        out_shape=pltpu.VMEM(gated.shape, jnp.bfloat16),
        cost_estimate=COST,
        compiler_params=params(),
        name="hidden_units",
    )(*in_vmem(gated, rows, w_up))


def units_kernel(*refs, parts):
    inputs, (w_gate, w_up), (hidden, rows) = refs[:parts], refs[parts : parts + 2], refs[-2:]
    held, _, units = w_gate.shape
    weights = gather_inputs(inputs, rows, held)
    for e in range(held):
        hidden[:, e * units : (e + 1) * units] = hidden_of(rows[...], w_gate[e], w_up[e], weights[e])


def units_of(parts, w_gate, w_up, *others):
    held, width, units = w_gate.shape
    count = sum(rows_in(part, width) for part in parts)
    return pl.pallas_call(
        functools.partial(units_kernel, parts=len(parts)),
        in_specs=[VMEM_SPEC] * (len(parts) + 2 + len(others)),
        out_specs=VMEM_SPEC,
        out_shape=pltpu.VMEM((count, held * units), jnp.bfloat16),
        scratch_shapes=[pltpu.VMEM((count, width), jnp.bfloat16)],
        cost_estimate=COST,
        compiler_params=params(),
        name="units_of",
    )(*in_vmem(*parts, w_gate, w_up, *others))


def both_kernel(gated, gated_rows, part, w_gate, w_up, first, second, rows):
    held, _, units = w_gate.shape
    weights = gather_inputs([part], rows, held)
    for e in range(held):
        block = slice(e * units, (e + 1) * units)
        up_act = jnp.dot(gated_rows[...], w_up[e], preferred_element_type=jnp.float32)
        first[:, block] = (gated[:, block] * up_act).astype(jnp.bfloat16)
        second[:, block] = hidden_of(rows[...], w_gate[e], w_up[e], weights[e])


def both_units(gated, gated_rows, part, w_gate, w_up):
    half = pltpu.VMEM(gated.shape, jnp.bfloat16)
    return pl.pallas_call(
        both_kernel,
        in_specs=[VMEM_SPEC] * 5,
        out_specs=[VMEM_SPEC] * 2,
        out_shape=[half, half],
        scratch_shapes=[pltpu.VMEM(gated_rows.shape, jnp.bfloat16)],
        cost_estimate=COST,
        compiler_params=params(),
        name="both_units",
    )(*in_vmem(gated, gated_rows, part, w_gate, w_up))


def rest_kernel(first, part, w_gate, w_up, w_down, mine, other, rows, hidden):
    held, _, units = w_gate.shape
    count = first.shape[0]
    weights = gather_inputs([part], rows, held)
    for e in range(held):
        block = slice(e * units, (e + 1) * units)
        hidden[:count, block] = first[:, block]
        hidden[count:, block] = hidden_of(rows[...], w_gate[e], w_up[e], weights[e])
    down_all(hidden, w_down, mine, other)


def rest_of(first, part, w_gate, w_up, w_down):
    held, width, units = w_gate.shape
    count = rows_in(part, width)
    return pl.pallas_call(
        rest_kernel,
        in_specs=[VMEM_SPEC] * 5,
        out_specs=[VMEM_SPEC] * 2,
        out_shape=[pltpu.VMEM((count, width), jnp.bfloat16)] * 2,
        scratch_shapes=[
            pltpu.VMEM((count, width), jnp.bfloat16),
            pltpu.VMEM((2 * count, held * units), jnp.bfloat16),
        ],
        cost_estimate=COST,
        compiler_params=params(),
        name="rest_of",
    )(*in_vmem(first, part, w_gate, w_up, w_down))


def sums_kernel(first, second, w_down, mine, *refs):
    *others, hidden = refs
    count = first.shape[0]
    hidden[:count] = first[...]
    hidden[count:] = second[...]
    down_all(hidden, w_down, mine, *others)


def sums_of(first, second, w_down, pieces=1):
    count, width = first.shape[0], w_down.shape[1]
    others = [pltpu.VMEM((count // pieces, width), jnp.bfloat16)] * pieces
    return pl.pallas_call(
        sums_kernel,
        in_specs=[VMEM_SPEC] * 3,
        out_specs=[VMEM_SPEC] * (1 + pieces),
        out_shape=[pltpu.VMEM((count, width), jnp.bfloat16), *others],
        scratch_shapes=[pltpu.VMEM((2 * count, first.shape[1]), jnp.bfloat16)],
        cost_estimate=COST,
        compiler_params=params(),
        name="sums_of",
    )(*in_vmem(first, second, w_down))


def pieces_kernel(mine, *refs):
    *others, out = refs
    piece = others[0].shape[0]
    for i, other in enumerate(others):
        rows = slice(i * piece, (i + 1) * piece)
        out[rows] = (mine[rows].astype(jnp.float32) + other[...].astype(jnp.float32)).astype(out.dtype)


def add_pieces(mine, others):
    return pl.pallas_call(
        pieces_kernel,
        in_specs=[VMEM_SPEC] * (1 + len(others)),
        out_specs=VMEM_SPEC,
        out_shape=pltpu.VMEM(mine.shape, mine.dtype),
        cost_estimate=COST,
        compiler_params=params(8),
        name="add_pieces",
    )(*in_vmem(mine, *others))


def down_units(hidden, w_down, pieces=1):
    count, width = hidden.shape[0] // 2, w_down.shape[1]
    others = [pltpu.VMEM((count // pieces, width), jnp.bfloat16)] * pieces
    return pl.pallas_call(
        down_all,
        in_specs=[VMEM_SPEC] * 2,
        out_specs=[VMEM_SPEC] * (1 + pieces),
        out_shape=[pltpu.VMEM((count, width), jnp.bfloat16), *others],
        cost_estimate=COST,
        compiler_params=params(),
        name="down_units",
    )(*in_vmem(hidden, w_down))


def add_kernel(*refs):
    *parts, out = refs
    width = parts[0].shape[1]
    total = parts[0][...].astype(jnp.float32)
    for part in parts[1:]:
        total += part[:, :width].astype(jnp.float32)
    out[:, :width] = total.astype(out.dtype)
    if out.shape[1] > width:
        out[:, width:] = jnp.zeros((out.shape[0], out.shape[1] - width), out.dtype)


def add(*parts, dtype=jnp.bfloat16, spare=0, cost=COST):
    count, width = parts[0].shape
    return pl.pallas_call(
        add_kernel,
        in_specs=[VMEM_SPEC] * len(parts),
        out_specs=VMEM_SPEC,
        out_shape=pltpu.VMEM((count, width + spare), dtype),
        cost_estimate=cost,
        compiler_params=params(8),
        name="add",
    )(*in_vmem(*parts))


def finish_kernel(*refs, pieces):
    *parts, out, block, sems = refs
    twins, parts = parts[:pieces], parts[pieces:]
    count = block.shape[1]
    copies = []
    for i in range(block.shape[0]):
        start = i * count
        rows = pl.ds(start, count)
        size = twins[0].shape[0]
        total = twins[start // size][pl.ds(start % size, count)].astype(jnp.float32)
        for part in parts:
            total += part[rows, : block.shape[2]].astype(jnp.float32)
        block[i] = total.astype(block.dtype)
        copies.append(pltpu.make_async_copy(block.at[i], out.at[rows], sems.at[i]))
        copies[-1].start()
    for copy in copies:
        copy.wait()


def finish(twins, *parts, blocks=4):
    count, width = parts[0].shape
    return pl.pallas_call(
        functools.partial(finish_kernel, pieces=len(twins)),
        in_specs=[VMEM_SPEC] * (len(twins) + len(parts)),
        out_specs=HBM_SPEC,
        out_shape=jax.ShapeDtypeStruct((count, width), jnp.bfloat16),
        scratch_shapes=[
            pltpu.VMEM((blocks, count // blocks, width), jnp.bfloat16),
            pltpu.SemaphoreType.DMA((blocks,)),
        ],
        cost_estimate=COST,
        compiler_params=params(8),
        name="finish",
    )(*in_vmem(*twins, *parts))


def on_four_chips(tokens, low, high, table, w_gate, w_up, w_down):
    x, y = 2, 4
    barrier = lax.optimization_barrier
    weights = (w_gate, w_up, w_down)
    near_rows, near_table = cross(tokens, x, y), cross(table, x, y)
    gated, rows = gated_units([low, high, flip(low, CORE), flip(high, CORE)], w_gate)
    wide = join(low, high, table, tokens.shape[1], SPARE)
    near_table, near_rows, gated, wide = barrier((near_table, near_rows, gated, wide))
    near = pack(near_rows, near_table)

    far = cross(near, y, x)
    mine_near, other_near = rest_of(units_of([near], *weights), flip(near, CORE), *weights)
    following = cross(wide, y, x)
    far, mine_near = barrier((far, mine_near))

    far_twin = flip(far, CORE)
    first = units_of([far], w_gate, w_up)
    first, far_twin = barrier((first, far_twin))
    second = units_of([far_twin], w_gate, w_up)
    mine_near, second = barrier((mine_near, second))
    sum_near = add(mine_near, flip(other_near, CORE), spare=LANES)
    back = cross(sum_near, x, y)
    following, second = barrier((following, second))
    mine_far, *other_far = sums_of(first, second, w_down)

    following_twin = flip(following, CORE)
    first, first_rows = gated_units([following], w_gate)
    mine_far, first = barrier((mine_far, first))
    sum_far = add_pieces(mine_far, [flip(other, CORE) for other in other_far])
    sum_far, following_twin, first = barrier((sum_far, following_twin, first))
    relay = cross(sum_far, x, y)
    first, second = both_units(first, first_rows, following_twin, w_gate, w_up)
    second, back = barrier((second, back))
    mine_last, other_last = sums_of(first, second, w_down)
    sum_last = add(add(mine_last, relay, dtype=jnp.float32, cost=RELAY), flip(other_last, CORE))
    last = cross(sum_last, y, x)
    hidden = hidden_units(gated, rows, w_up)
    mine_own, *other_own = down_units(hidden, w_down, pieces=2)
    return finish([flip(other, CORE) for other in other_own], mine_own, back, last)


def on_any_chips(tokens, low, high, table, *weights):
    own = join(low, high, table, tokens.shape[1])
    offsets = range(2, lax.axis_size("ep"), 2)
    arrived = [flip(own, d) for d in offsets]
    parts = []
    for d, rows in zip([0, *offsets], [own, *arrived]):
        mine, other = rest_of(units_of([rows], *weights[:2]), flip(rows, CORE), *weights)
        other = flip(other, CORE)
        parts += [flip(add(mine, other), d)] if d else [mine, other]
    return finish(parts[:1], *parts[1:])


def body(tokens, experts, gates, w_gate, w_up, w_down):
    n_ep = lax.axis_size("ep")
    n_experts = w_gate.shape[0] * n_ep
    packed = prepare(tokens, experts, gates, n_experts)
    run = on_four_chips if n_ep == 8 else on_any_chips
    return run(tokens, *packed, w_gate, w_up, w_down)


def solution(mesh):
    in_specs = (
        P(("rep", "ep"), None),
        P(("rep", "ep"), None),
        P(("rep", "ep"), None),
        P("ep", None, None),
        P("ep", None, None),
        P("ep", None, None),
    )
    out_specs = P(("rep", "ep"), None)
    return jax.shard_map(body, mesh=mesh, in_specs=in_specs, out_specs=out_specs, check_vma=False)
```
